256 devices in a mesh: dp: 16 (over z, core), mp: 16 (over x, y).
Axes of the slice: x: 4, y: 4, z: 8, core: 2. Of those that a mesh axis runs over, the one named last changes fastest.
Arguments:
- tokens: bfloat16 [12288, 2304], P('dp'), may hold values from -6 to 6
- up_cotangent: bfloat16 [12288, 18432], P('dp', 'mp'), may hold values from -0.59765625 to 0.59765625
- up_weight: bfloat16 [2304, 18432], P('dp', 'mp'), may hold values from -0.1875 to 0.1875
- carried: bfloat16 [16, 2304, 18432], P('dp', None, 'mp'), may hold values from -12 to 12
- momentum: float32 [2304, 18432], P('dp', 'mp'), may hold values from -3 to 3
- q_start: float32 [18432, 64], P('mp'), may hold values from -6 to 6
Outputs:
- feature_grad: float32 [12288, 2304], P('dp', 'mp')
- right_factor: float32 [18432, 64], P('mp')
- new_momentum: float32 [2304, 18432], P('dp', 'mp')
The draws below stay inside these ranges and needn't reach their ends.
All inputs are finite; a program needn't handle non-finite values.
Results may differ from the reference program's by a relative error of at most 0.0003.
Values may be sent and summed in bfloat16 or wider, within the bound.
A program may use at most 128 MiB of HBM per device.

```python
import jax
import jax.numpy as jnp
from jax import lax

D = 2304
FF_DEV = 1152
RANK = 64
TOK_DEV = 768
TOKENS = 12288
FF = 18432
N_DP = 16
N_MP = 16


def raised(entries, own_key, source, target, blocks, factor):
    def block_of(dim):
        return (jnp.arange(entries.shape[dim]) // (entries.shape[dim] // blocks)).reshape((-1,) + (1,) * (entries.ndim - 1 - dim))

    one_side = jax.random.permutation(own_key, blocks)[block_of(target)]
    second = (block_of(target) + blocks // 2) % blocks
    return jnp.where((block_of(source) == one_side) | (block_of(source) == second), factor * entries, entries)


def shard_levels(key, shape, split, smallest, top_value):
    factor_of = 1.0
    for position, shards_of in split:
        heights = jax.random.uniform(jax.random.fold_in(jax.random.fold_in(key, 6), position), (shards_of,), jnp.float32, smallest / len(split), top_value / len(split))
        factor_of = factor_of * jnp.repeat(jnp.exp(heights), shape[position] // shards_of).reshape((-1,) + (1,) * (len(shape) - 1 - position))
    return factor_of


def noise(rng, extent, deviation, reach, split=(), kind=jnp.bfloat16):
    array = jax.random.normal(rng, extent, jnp.float32) * deviation
    if len(split) > 0:
        array = shard_levels(rng, extent, split, -0.22, 0.18) * array
    return jnp.clip(array, min=-reach, max=reach).astype(kind)


def gaussian_with(own_key, extent, width, limit, cuts, heavy, held_as=jnp.bfloat16):
    entries = width * jax.random.normal(own_key, extent, jnp.float32)
    if cuts:
        entries = entries * shard_levels(own_key, extent, cuts, -0.22, 0.18)
    return jnp.clip(raised(entries, jax.random.fold_in(own_key, 3), *heavy), -limit, limit).astype(held_as)


def setup_inputs(seed: int = 0) -> dict:
    key_of = jax.random.split(jax.random.key(seed), 7)
    return {
        "tokens": noise(key_of[0], (TOKENS, D), 1.0, 6.0, ((0, 16),)),
        "up_cotangent": noise(key_of[1], (TOKENS, FF), 0.1, 0.59765625, ((0, 16), (1, 16))),
        "up_weight": noise(key_of[2], (D, FF), FF_DEV ** -0.5, 0.1875, ((0, 16), (1, 16))),
        "carried": gaussian_with(key_of[3], (N_DP, D, FF), 2.0, 12.0, ((0, 16), (2, 16)), (0, 1, 16, 2.0)),
        "momentum": noise(key_of[4], (D, FF), 0.5, 3.0, ((0, 16), (1, 16)), jnp.float32),
        "q_start": noise(key_of[5], (FF, RANK), 1.0, 6.0, ((0, 16),), jnp.float32),
    }


decay_rate = 0.9

def orthonormal(left):
    gram = jnp.dot(left.T, left, precision=lax.Precision.HIGHEST)
    lower = jnp.linalg.cholesky(gram)
    return jax.scipy.linalg.solve_triangular(lower, left.T, lower=True).T

def reference(tokens, up_cotangent, up_weight, carried, momentum, q_start):
    feature_grad = jnp.dot(up_cotangent.astype(jnp.float32), up_weight.T.astype(jnp.float32), preferred_element_type=jnp.float32)
    replica_tokens = tokens.astype(jnp.float32).reshape(N_DP, TOK_DEV, D)

    def one_block(block):
        first = (block * FF_DEV).astype(jnp.int32)
        cot = lax.dynamic_slice_in_dim(up_cotangent, first, FF_DEV, 1)
        cot = cot.astype(jnp.float32).reshape(N_DP, TOK_DEV, FF_DEV)
        error = lax.dynamic_slice_in_dim(carried, first, FF_DEV, 2).astype(jnp.float32)
        start = lax.dynamic_slice_in_dim(q_start, first, FF_DEV, 0)
        grads = jnp.einsum('rtd,rtf->rdf', replica_tokens, cot, precision=lax.Precision.HIGHEST)
        whole = error + grads
        left = jnp.einsum('rdf,fk->dk', whole, start, precision=lax.Precision.HIGHEST) / N_DP
        basis = orthonormal(left)
        right = jnp.einsum('rdf,dk->fk', whole, basis, precision=lax.Precision.HIGHEST) / N_DP
        decoded = jnp.dot(basis, right.T, precision=lax.Precision.HIGHEST)
        previous = lax.dynamic_slice_in_dim(momentum, first, FF_DEV, 1)
        return (right, decay_rate * previous + decoded)
    rights, moments = lax.map(one_block, jnp.arange(N_MP, dtype=jnp.int32))
    right_factor = rights.reshape(FF, RANK)
    new_momentum = jnp.transpose(moments, (1, 0, 2)).reshape(D, FF)
    return (feature_grad, right_factor, new_momentum)
```

```python
import jax
import jax.numpy as jnp
from jax import lax
from jax.experimental import pallas as pl
from jax.experimental.pallas import tpu as pltpu
from jax.sharding import PartitionSpec as P

DECAY = 0.9
MESH = pl.DeviceIdType.MESH
NT = (((1,), (1,)), ((), ()))
NN = (((1,), (0,)), ((), ()))
TN = (((0,), (0,)), ((), ()))
NZ = 8
NDP = 16
RANK = 64
TILE = 384
FAR_FIRST = (4, 3, 5, 2, 6, 1, 7)


def mm(a, b, dims):
    return lax.dot_general(a, b, dims, preferred_element_type=jnp.float32)


def mm32(a, b, dims):
    return lax.dot_general(
        a, b, dims, precision=lax.Precision.HIGHEST, preferred_element_type=jnp.float32
    )


def split3(x):
    hi = x.astype(jnp.bfloat16)
    rest = x - hi.astype(jnp.float32)
    mid = rest.astype(jnp.bfloat16)
    low = (rest - mid.astype(jnp.float32)).astype(jnp.bfloat16)
    return jnp.concatenate([hi, mid, low], axis=0)


def fold3(x):
    return x[0:RANK] + x[RANK : 2 * RANK] + x[2 * RANK :]


def aligned(i, n):
    return pl.multiple_of(i * n, n)


def compress_kernel(
    tokens_hbm, cot_hbm, carried_hbm, momentum_hbm, q_ref,
    right_ref, mom_ref,
    tokens, cot, carried, momentum, q3, t3, lp, sib_l, cs, rsl, left, left3,
    yp, sib_y, ys, rsy, yf, elim,
    load_sem, sib_sem, rs_s, rs_r, ag_s, ag_r, yrs_s, yrs_r, yag_s, yag_r,
):
    dp = lax.axis_index("dp")
    mp = lax.axis_index("mp")
    z, c = dp // 2, dp % 2
    sib = (z * 2 + 1 - c, mp)

    def zdev(d):
        return ((z + d) % NZ * 2 + c, mp)

    loads = [
        pltpu.make_async_copy(src, dst, load_sem.at[i])
        for i, (src, dst) in enumerate(
            ((cot_hbm, cot), (tokens_hbm, tokens), (carried_hbm, carried), (momentum_hbm, momentum))
        )
    ]
    for copy in loads:
        copy.start()
    barrier = pltpu.get_barrier_semaphore()
    pl.semaphore_signal(barrier, inc=1, device_id=sib, device_id_type=MESH)
    for d in range(1, NZ):
        pl.semaphore_signal(barrier, inc=1, device_id=zdev(d), device_id_type=MESH)

    q3[...] = split3(q_ref[...])
    loads[0].wait()
    for t in range(2):
        rows = pl.ds(t * TILE, TILE)
        t3[:, rows] = split3(fold3(mm(q3[...], cot[rows, :], NT)))
    loads[1].wait()
    loads[2].wait()

    def left_tile(t, _):
        columns = pl.ds(aligned(t, TILE), TILE)
        part = mm(q3[...], carried[columns, :], NT) + mm(t3[...], tokens[:, columns], NN)
        lp[t // 3, :, pl.ds(aligned(t % 3, TILE), TILE)] = fold3(part)
        return 0

    lax.fori_loop(0, 6, left_tile, 0)
    pl.semaphore_wait(barrier, NZ)

    def exchange(src, dst, slot):
        return pltpu.make_async_remote_copy(
            src_ref=src, dst_ref=dst, send_sem=sib_sem.at[2 * slot], recv_sem=sib_sem.at[2 * slot + 1],
            device_id=sib, device_id_type=MESH,
        )

    def scatter(src, dst, send, recv):
        copies = []
        for d in FAR_FIRST:
            copy = pltpu.make_async_remote_copy(
                src_ref=src.at[pl.ds(aligned((z + d) % NZ, 8), 8), :], dst_ref=dst.at[d],
                send_sem=send.at[d], recv_sem=recv.at[d], device_id=zdev(d), device_id_type=MESH,
            )
            copy.start()
            copies.append(copy)
        return copies

    def gather(block_of, send, recv):
        copies, arrivals = [], []
        for d in FAR_FIRST:
            copy = pltpu.make_async_remote_copy(
                src_ref=block_of(z), dst_ref=block_of(z),
                send_sem=send.at[d], recv_sem=recv.at[d], device_id=zdev(d), device_id_type=MESH,
            )
            copy.start()
            copies.append(copy)
            arrivals.append(
                pltpu.make_async_remote_copy(
                    src_ref=block_of(z), dst_ref=block_of((z - d + NZ) % NZ),
                    send_sem=send.at[d], recv_sem=recv.at[d], device_id=zdev(d), device_id_type=MESH,
                )
            )
        return copies, arrivals

    pair = exchange(lp.at[1 - c], sib_l, 0)
    pair.start()
    pair.wait()
    cs[...] = lp[c] + sib_l[...]
    copies = scatter(cs, rsl, rs_s, rs_r)
    own_rows = pl.ds(aligned(z, 8), 8)
    total = cs[own_rows, :]
    for copy in copies:
        copy.wait_recv()
    for d in range(1, NZ):
        total = total + rsl[d]
    left[c, own_rows, :] = total * (1.0 / NDP)
    for copy in copies:
        copy.wait_send()
    copies, arrivals = gather(lambda j: left.at[c, pl.ds(aligned(j, 8), 8), :], ag_s, ag_r)
    for copy in arrivals:
        copy.wait_recv()
    for copy in copies:
        copy.wait_send()
    pair = exchange(left.at[c], left.at[c], 1)
    pair.start()
    back = exchange(left.at[c], left.at[1 - c], 1)
    back.wait_recv()
    pair.wait_send()

    for h in range(2):
        left3[:, h * 1152 : (h + 1) * 1152] = split3(left[h])
    for t in range(2):
        rows = pl.ds(t * TILE, TILE)
        t3[:, rows] = split3(fold3(mm(left3[...], tokens[rows, :], NT)))

    def y_tile(t, _):
        columns = pl.ds(aligned(t, TILE), TILE)
        part = mm(left3[...], carried[:, columns], NN) + mm(t3[...], cot[:, columns], NN)
        yp[:, columns] = fold3(part)
        return 0

    lax.fori_loop(0, 3, y_tile, 0)

    def mine(core):
        return pl.ds(pl.multiple_of(core * 512, 128), 640)

    pair = exchange(yp.at[:, mine(1 - c)], sib_y, 2)
    pair.start()
    pair.wait()
    ys[...] = yp[:, mine(c)] + sib_y[...]
    copies = scatter(ys, rsy, yrs_s, yrs_r)

    products = mm(left3[...], left3[...], NT)
    gram = jnp.zeros((RANK, RANK), jnp.float32)
    for i in (2, 1, 0):
        for j in (2, 1, 0):
            gram = gram + products[i * RANK : (i + 1) * RANK, j * RANK : (j + 1) * RANK]
    row_id = lax.broadcasted_iota(jnp.int32, (RANK, 2 * RANK), 0)
    lane_id = lax.broadcasted_iota(jnp.int32, (RANK, 2 * RANK), 1)
    elim[:, 0:RANK] = gram
    elim[:, RANK:] = jnp.where(row_id[:, 0:RANK] == lane_id[:, 0:RANK], 1.0, 0.0)

    def eliminate(j, _):
        row = elim[pl.ds(j, 1), :]
        full = elim[...]
        pivot = jnp.sum(jnp.where(lane_id[0:1] == j, row, 0.0), axis=1, keepdims=True)
        column = jnp.sum(jnp.where(lane_id == j, full, 0.0), axis=1, keepdims=True)
        factor = jnp.where(row_id[:, 0:1] > j, column / pivot, 0.0)
        elim[...] = full - factor * row
        return 0

    lax.fori_loop(0, RANK - 1, eliminate, 0)
    done = elim[...]
    diagonal = jnp.sum(jnp.where(lane_id == row_id, done, 0.0), axis=1, keepdims=True)
    inverse = done[:, RANK:] / jnp.sqrt(diagonal)
    k = dp % 8
    window = left[dp // 8, :, pl.ds(aligned(k, 128), 256)]
    own_left = pltpu.roll(window, (256 - 16 * k) % 256, 1)[:, 0:144]
    own_basis = mm32(inverse, own_left, NN)

    total = ys[own_rows, :]
    for copy in copies:
        copy.wait_recv()
    for d in range(1, NZ):
        total = total + rsy[d]
    yf[own_rows, mine(c)] = total
    for copy in copies:
        copy.wait_send()
    copies, arrivals = gather(lambda j: yf.at[pl.ds(aligned(j, 8), 8), mine(c)], yag_s, yag_r)
    for copy in arrivals:
        copy.wait_recv()
    for copy in copies:
        copy.wait_send()

    def given(core):
        return yf.at[:, pl.ds(pl.multiple_of(core * 640, 128), 512)]

    pair = exchange(given(c), given(c), 3)
    pair.start()
    back = exchange(given(c), given(1 - c), 3)
    back.wait_recv()
    pair.wait_send()
    loads[3].wait()
    for t in range(3):
        columns = pl.ds(t * TILE, TILE)
        right = mm32(inverse, yf[:, columns], NN) * (1.0 / NDP)
        right_ref[:, columns] = right
        mom_ref[:, columns] = DECAY * momentum[:, columns] + mm32(own_basis, right, TN)


def compress(tokens, cot, carried, momentum, q_t):
    f32, bf16 = jnp.float32, jnp.bfloat16
    dma = pltpu.SemaphoreType.DMA
    hbm = pl.BlockSpec(memory_space=pl.ANY)
    vmem = pl.BlockSpec(memory_space=pltpu.VMEM)
    return pl.pallas_call(
        compress_kernel,
        out_shape=(
            jax.ShapeDtypeStruct((RANK, 1152), f32),
            jax.ShapeDtypeStruct((144, 1152), f32),
        ),
        in_specs=[hbm] * 4 + [vmem],
        out_specs=(vmem, vmem),
        scratch_shapes=[
            pltpu.VMEM((768, 2304), bf16),
            pltpu.VMEM((768, 1152), bf16),
            pltpu.VMEM((2304, 1152), bf16),
            pltpu.VMEM((144, 1152), f32),
            pltpu.VMEM((192, 1152), bf16),
            pltpu.VMEM((192, 768), bf16),
            pltpu.VMEM((2, RANK, 1152), f32),
            pltpu.VMEM((RANK, 1152), f32),
            pltpu.VMEM((RANK, 1152), f32),
            pltpu.VMEM((NZ, 8, 1152), f32),
            pltpu.VMEM((2, RANK, 1152), f32),
            pltpu.VMEM((192, 2304), bf16),
            pltpu.VMEM((RANK, 1152), f32),
            pltpu.VMEM((RANK, 640), f32),
            pltpu.VMEM((RANK, 640), f32),
            pltpu.VMEM((NZ, 8, 640), f32),
            pltpu.VMEM((RANK, 1152), f32),
            pltpu.VMEM((RANK, 128), f32),
            dma((4,)),
            dma((8,)),
        ]
        + [dma((NZ,))] * 8,
        compiler_params=pltpu.CompilerParams(
            collective_id=0, has_side_effects=True, vmem_limit_bytes=48 * 2**20
        ),
        cost_estimate=pl.CostEstimate(
            flops=4 * 10**9, bytes_accessed=12 * 10**6, transcendentals=0
        ),
        name="compress",
    )(tokens, cot, carried, momentum, q_t)


def body(tokens, up_cotangent, up_weight, carried, momentum, q_start):
    partial_value = lax.dot_general(
        up_cotangent,
        lax.all_gather(up_weight, "dp", axis=0, tiled=True),
        (((1,), (1,)), ((), ())),
        preferred_element_type=jnp.float32,
    )
    feature_grad = lax.psum_scatter(partial_value, "mp", scatter_dimension=1, tiled=True)
    right_t, new_momentum = compress(tokens, up_cotangent, carried[0], momentum, q_start.T)
    return (feature_grad, right_t.T, new_momentum)


def solution(mesh):
    placed = (
        P("dp", None),
        P("dp", "mp"),
        P("dp", "mp"),
        P("dp", None, "mp"),
        P("dp", "mp"),
        P("mp", None),
    )
    return jax.shard_map(
        body,
        mesh=mesh,
        in_specs=placed,
        out_specs=(P("dp", "mp"), P("mp", None), P("dp", "mp")),
        check_vma=False,
    )
```

```python
import jax
import jax.numpy as jnp
from jax import lax
from jax.experimental import pallas as pl
from jax.experimental.pallas import tpu as pltpu
from jax.sharding import PartitionSpec as P

DECAY = 0.9
MESH = pl.DeviceIdType.MESH
NT = (((1,), (1,)), ((), ()))
NN = (((1,), (0,)), ((), ()))
TN = (((0,), (0,)), ((), ()))
NZ = 8
NDP = 16
RANK = 64
TILE = 384
FAR_FIRST = (4, 3, 5, 2, 6, 1, 7)
CHUNK = 144
HALF = 72
SPLIT = 80


def mm(a, b, dims):
    return lax.dot_general(a, b, dims, preferred_element_type=jnp.float32)


def mm32(a, b, dims):
    return lax.dot_general(
        a, b, dims, precision=lax.Precision.HIGHEST, preferred_element_type=jnp.float32
    )


def split3(x):
    hi = x.astype(jnp.bfloat16)
    rest = x - hi.astype(jnp.float32)
    mid = rest.astype(jnp.bfloat16)
    low = (rest - mid.astype(jnp.float32)).astype(jnp.bfloat16)
    return jnp.concatenate([hi, mid, low], axis=0)


def fold3(x):
    return x[0:RANK] + x[RANK : 2 * RANK] + x[2 * RANK :]


def aligned(i, n):
    return pl.multiple_of(i * n, n)


def fused_kernel(
    tokens_hbm, cot_hbm, weight_hbm, carried_hbm, momentum_hbm, q_ref,
    feature_ref, right_ref, mom_ref,
    tokens, cot, carried, momentum, q3, t3, lp, sib_l, cs, rsl, left, left3,
    yp, sib_y, ys, rsy, yf, elim,
    weight, part, r1, rl1, r2, rl2,
    load_sem, sib_sem, rs_s, rs_r, ag_s, ag_r, yrs_s, yrs_r, yag_s, yag_r,
    w_s, w_r, ws_s, ws_r, f1_s, r1_r, rl1_r, f2_s, r2_r, rl2_r,
):
    dp = lax.axis_index("dp")
    mp = lax.axis_index("mp")
    z, c = dp // 2, dp % 2
    x, y = mp // 4, mp % 4
    sib = (z * 2 + 1 - c, mp)

    def zdev(d):
        return ((z + d) % NZ * 2 + c, mp)

    def xydev(axis, d):
        if axis == 0:
            return (dp, (x + d) % 4 * 4 + y)
        return (dp, x * 4 + (y + d) % 4)

    def remote(src, dst, send, recv, device):
        return pltpu.make_async_remote_copy(
            src_ref=src, dst_ref=dst, send_sem=send, recv_sem=recv,
            device_id=device, device_id_type=MESH,
        )

    own_chunk = pl.ds(pl.multiple_of(dp * CHUNK, 16), CHUNK)
    loads = [
        pltpu.make_async_copy(src, dst, load_sem.at[i])
        for i, (src, dst) in enumerate(
            (
                (weight_hbm, weight.at[own_chunk, :]), (cot_hbm, cot), (tokens_hbm, tokens),
                (carried_hbm, carried), (momentum_hbm, momentum),
            )
        )
    ]
    for copy in loads:
        copy.start()
    barrier = pltpu.get_barrier_semaphore()
    pl.semaphore_signal(barrier, inc=1, device_id=sib, device_id_type=MESH)
    for d in FAR_FIRST:
        pl.semaphore_signal(barrier, inc=1, device_id=zdev(d), device_id_type=MESH)
    for axis in range(2):
        for d in (1, 3):
            pl.semaphore_signal(barrier, inc=1, device_id=xydev(axis, d), device_id_type=MESH)

    def weight_rows(way, s, core, first=0, count=CHUNK):
        place = (z - s + NZ) % NZ if way == 0 else (z + s) % NZ
        return weight.at[pl.ds(pl.multiple_of((place * 2 + core) * CHUNK + first, 16), count), :]

    def ring_copy(way, s):
        first, count = 0, CHUNK
        if s == 4:
            first, count = (0, SPLIT) if way == 0 else (SPLIT, CHUNK - SPLIT)
        src = weight_rows(way, s - 1, c, first, count)
        return remote(src, src, w_s.at[way, s - 1], w_r.at[way, s], zdev(1 if way == 0 else NZ - 1))

    def ring_arrival(way, s):
        first, count = 0, CHUNK
        if s == 4:
            first, count = (0, SPLIT) if way == 0 else (SPLIT, CHUNK - SPLIT)
        dst = weight_rows(way, s, c, first, count)
        return remote(dst, dst, w_s.at[way, s - 1], w_r.at[way, s], zdev(1))

    def pair_copy(way, s, core):
        rows = weight_rows(way, s, core)
        return remote(rows, rows, ws_s.at[way, s], ws_r.at[way, s], sib)

    def ways_of(s):
        return (0,) if s in (0, 4) else (0, 1)

    def ring_step(s):
        for way in (0, 1):
            if s > 0:
                ring_arrival(way, s).wait_recv()
            if s < 4:
                ring_copy(way, s + 1).start()
            if s in (1, 2, 3):
                pair_copy(way, s, c).start()
        if s in (0, 4):
            pair_copy(0, s, c).start()

    def block(h, j, upper):
        return part.at[h, pl.ds(pl.multiple_of(j * CHUNK + (0 if upper else HALF), 8), HALF), :]

    def rows_of(upper):
        return pl.ds(0 if upper else HALF, HALF)

    class Stage:
        def __init__(self, number):
            self.number = number
            self.sends, self.arrive, self.passed = ((f1_s, r1_r, rl1_r), (f2_s, r2_r, rl2_r))[number]
            self.into, self.relay = ((r1, rl1), (r2, rl2))[number]

        def axis(self, h):
            return h if self.number == 0 else 1 - h

        def slot(self, h, j):
            if self.number == 1:
                return 0
            return j % 4 if h == 0 else j // 4

        def distance(self, h, j):
            if self.axis(h) == 0:
                return (j // 4 - x + 4) % 4
            return (j % 4 - y + 4) % 4

        def send(self, h, j, upper, direct, way):
            k = self.slot(h, j)
            source = block(h, j, upper)
            part_id = 0 if upper else 1
            if direct:
                dst = self.into.at[h, way, k, rows_of(upper), :]
                recv = self.arrive.at[h, way, k, part_id]
            else:
                dst = self.relay.at[h, way, k]
                recv = self.passed.at[h, way, k]
            return remote(
                source, dst, self.sends.at[h, j, part_id], recv,
                xydev(self.axis(h), 1 if way == 0 else 3),
            )

        def plain(self, h, j):
            far = self.distance(h, j)

            @pl.when(far == 2)
            def _():
                self.send(h, j, True, False, 0).start()
                self.send(h, j, False, False, 1).start()

            @pl.when(far == 1)
            def _():
                self.send(h, j, False, True, 0).start()

            @pl.when(far == 3)
            def _():
                self.send(h, j, True, True, 1).start()

        def merge(self, h, j):
            far = self.distance(h, j)
            k = self.slot(h, j)

            def one(way, upper):
                rows = block(h, j, upper)
                copy = remote(
                    self.relay.at[h, way, k], self.relay.at[h, way, k],
                    self.sends.at[h, j, 0], self.passed.at[h, way, k], xydev(self.axis(h), 1),
                )
                copy.wait_recv()
                rows[...] = rows[...] + self.relay[h, way, k]
                self.send(h, j, upper, True, way).start()

            @pl.when(far == 1)
            def _():
                one(0, True)

            @pl.when(far == 3)
            def _():
                one(1, False)

        def collect(self, h, j):
            k = self.slot(h, j)
            for way in range(2):
                for upper in (True, False):
                    dst = self.into.at[h, way, k, rows_of(upper), :]
                    remote(
                        dst, dst, self.sends.at[h, j, 0],
                        self.arrive.at[h, way, k, 0 if upper else 1], xydev(self.axis(h), 1),
                    ).wait_recv()
            own = pl.ds(pl.multiple_of(j * CHUNK, 8), CHUNK)
            return part[h, own, :] + self.into[h, 0, k] + self.into[h, 1, k]

        def drain(self, h, j):
            @pl.when(self.distance(h, j) != 0)
            def _():
                for upper in (True, False):
                    self.send(h, j, upper, True, 0).wait_send()

    first, second = Stage(0), Stage(1)

    def place_of(way, s):
        return (z - s + NZ) % NZ if way == 0 else (z + s) % NZ

    def partials(s):
        for way in ways_of(s):
            place = place_of(way, s)
            pair_copy(way, s, 1 - c).wait_recv()
            rows = pl.ds(pl.multiple_of(place * (2 * CHUNK), 16), 2 * CHUNK)
            for h in range(2):
                part[h, rows, :] = mm(weight[rows, :], cot[pl.ds(h * TILE, TILE), :], NT)
            for h in range(2):
                for b in range(2):
                    first.plain(h, place * 2 + b)

    def merges(s):
        for way in ways_of(s):
            for b in range(2):
                for h in range(2):
                    first.merge(h, place_of(way, s) * 2 + b)

    def own_block(h, k):
        return x * 4 + k if h == 0 else k * 4 + y

    def second_start():
        for k in range(4):
            for h in range(2):
                j = own_block(h, k)
                total = first.collect(h, j)
                part[h, pl.ds(pl.multiple_of(j * CHUNK, 8), CHUNK), :] = total
                second.plain(h, j)

    def second_merges():
        for k in range(4):
            for h in range(2):
                second.merge(h, own_block(h, k))

    def feature_finish():
        for h in range(2):
            feature_ref[:, pl.ds(h * TILE, TILE)] = second.collect(h, mp)

    q3[...] = split3(q_ref[...])
    loads[1].wait()
    for t in range(2):
        rows = pl.ds(t * TILE, TILE)
        t3[:, rows] = split3(fold3(mm(q3[...], cot[rows, :], NT)))
    loads[0].wait()
    pl.semaphore_wait(barrier, NZ + 4)
    ring_step(0)

    loads[2].wait()
    loads[3].wait()

    def left_tile(t, _):
        columns = pl.ds(aligned(t, TILE), TILE)
        value = mm(q3[...], carried[columns, :], NT) + mm(t3[...], tokens[:, columns], NN)
        lp[t // 3, :, pl.ds(aligned(t % 3, TILE), TILE)] = fold3(value)
        return 0

    lax.fori_loop(0, 6, left_tile, 0)

    def exchange(src, dst, slot):
        return remote(src, dst, sib_sem.at[2 * slot], sib_sem.at[2 * slot + 1], sib)

    def scatter(src, dst, send, recv):
        copies = []
        for d in FAR_FIRST:
            copy = remote(
                src.at[pl.ds(aligned((z + d) % NZ, 8), 8), :], dst.at[d],
                send.at[d], recv.at[d], zdev(d),
            )
            copy.start()
            copies.append(copy)
        return copies

    def gather(block_of, send, recv):
        copies, arrivals = [], []
        for d in FAR_FIRST:
            copy = remote(block_of(z), block_of(z), send.at[d], recv.at[d], zdev(d))
            copy.start()
            copies.append(copy)
            arrivals.append(
                remote(block_of(z), block_of((z - d + NZ) % NZ), send.at[d], recv.at[d], zdev(d))
            )
        return copies, arrivals

    pair = exchange(lp.at[1 - c], sib_l, 0)
    pair.start()
    partials(0)
    pair.wait()
    cs[...] = lp[c] + sib_l[...]
    copies = scatter(cs, rsl, rs_s, rs_r)
    ring_step(1)
    partials(1)
    merges(0)
    own_rows = pl.ds(aligned(z, 8), 8)
    total = cs[own_rows, :]
    for copy in copies:
        copy.wait_recv()
    for d in range(1, NZ):
        total = total + rsl[d]
    left[c, own_rows, :] = total * (1.0 / NDP)
    for copy in copies:
        copy.wait_send()
    copies, arrivals = gather(lambda j: left.at[c, pl.ds(aligned(j, 8), 8), :], ag_s, ag_r)
    ring_step(2)
    partials(2)
    merges(1)
    for copy in arrivals:
        copy.wait_recv()
    for copy in copies:
        copy.wait_send()
    pair = exchange(left.at[c], left.at[c], 1)
    pair.start()
    ring_step(3)
    exchange(left.at[c], left.at[1 - c], 1).wait_recv()
    pair.wait_send()

    for h in range(2):
        left3[:, h * 1152 : (h + 1) * 1152] = split3(left[h])
    for t in range(2):
        rows = pl.ds(t * TILE, TILE)
        t3[:, rows] = split3(fold3(mm(left3[...], tokens[rows, :], NT)))

    def y_tile(t, _):
        columns = pl.ds(aligned(t, TILE), TILE)
        value = mm(left3[...], carried[:, columns], NN) + mm(t3[...], cot[:, columns], NN)
        yp[:, columns] = fold3(value)
        return 0

    lax.fori_loop(0, 3, y_tile, 0)

    def mine(core):
        return pl.ds(pl.multiple_of(core * 512, 128), 640)

    pair = exchange(yp.at[:, mine(1 - c)], sib_y, 2)
    pair.start()
    partials(3)
    merges(2)
    pair.wait()
    ys[...] = yp[:, mine(c)] + sib_y[...]
    copies = scatter(ys, rsy, yrs_s, yrs_r)
    ring_step(4)
    partials(4)
    merges(3)

    products = mm(left3[...], left3[...], NT)
    gram = jnp.zeros((RANK, RANK), jnp.float32)
    for i in (2, 1, 0):
        for j in (2, 1, 0):
            gram = gram + products[i * RANK : (i + 1) * RANK, j * RANK : (j + 1) * RANK]
    row_id = lax.broadcasted_iota(jnp.int32, (RANK, 2 * RANK), 0)
    lane_id = lax.broadcasted_iota(jnp.int32, (RANK, 2 * RANK), 1)
    elim[:, 0:RANK] = gram
    elim[:, RANK:] = jnp.where(row_id[:, 0:RANK] == lane_id[:, 0:RANK], 1.0, 0.0)

    def eliminate(j, _):
        row = elim[pl.ds(j, 1), :]
        full = elim[...]
        pivot = jnp.sum(jnp.where(lane_id[0:1] == j, row, 0.0), axis=1, keepdims=True)
        column = jnp.sum(jnp.where(lane_id == j, full, 0.0), axis=1, keepdims=True)
        factor = jnp.where(row_id[:, 0:1] > j, column / pivot, 0.0)
        elim[...] = full - factor * row
        return 0

    lax.fori_loop(0, RANK - 1, eliminate, 0)

    total = ys[own_rows, :]
    for copy in copies:
        copy.wait_recv()
    for d in range(1, NZ):
        total = total + rsy[d]
    yf[own_rows, mine(c)] = total
    for copy in copies:
        copy.wait_send()
    copies, arrivals = gather(lambda j: yf.at[pl.ds(aligned(j, 8), 8), mine(c)], yag_s, yag_r)
    merges(4)
    done = elim[...]
    diagonal = jnp.sum(jnp.where(lane_id == row_id, done, 0.0), axis=1, keepdims=True)
    inverse = done[:, RANK:] / jnp.sqrt(diagonal)
    k = dp % 8
    window = left[dp // 8, :, pl.ds(aligned(k, 128), 256)]
    own_left = pltpu.roll(window, (256 - 16 * k) % 256, 1)[:, 0:CHUNK]
    own_basis = mm32(inverse, own_left, NN)
    second_start()
    for copy in arrivals:
        copy.wait_recv()
    for copy in copies:
        copy.wait_send()

    def given(core):
        return yf.at[:, pl.ds(pl.multiple_of(core * 640, 128), 512)]

    pair = exchange(given(c), given(c), 3)
    pair.start()
    second_merges()
    exchange(given(c), given(1 - c), 3).wait_recv()
    pair.wait_send()
    loads[4].wait()
    for t in range(3):
        columns = pl.ds(t * TILE, TILE)
        right = mm32(inverse, yf[:, columns], NN) * (1.0 / NDP)
        right_ref[:, columns] = right
        mom_ref[:, columns] = DECAY * momentum[:, columns] + mm32(own_basis, right, TN)
    feature_finish()

    for s in range(5):
        for way in (0, 1):
            if s < 4:
                ring_copy(way, s + 1).wait_send()
            if way in ways_of(s):
                pair_copy(way, s, c).wait_send()

    def drain(j, _):
        for h in range(2):
            first.drain(h, j)
        return 0

    lax.fori_loop(0, NDP, drain, 0)

    def drain_second(k, _):
        for h in range(2):
            second.drain(h, own_block(h, k))
        return 0

    lax.fori_loop(0, 4, drain_second, 0)


def fused(tokens, cot, weight, carried, momentum, q_t):
    f32, bf16 = jnp.float32, jnp.bfloat16
    dma = pltpu.SemaphoreType.DMA
    hbm = pl.BlockSpec(memory_space=pl.ANY)
    vmem = pl.BlockSpec(memory_space=pltpu.VMEM)
    return pl.pallas_call(
        fused_kernel,
        out_shape=(
            jax.ShapeDtypeStruct((CHUNK, 768), f32),
            jax.ShapeDtypeStruct((RANK, 1152), f32),
            jax.ShapeDtypeStruct((CHUNK, 1152), f32),
        ),
        in_specs=[hbm] * 5 + [vmem],
        out_specs=(vmem, vmem, vmem),
        scratch_shapes=[
            pltpu.VMEM((768, 2304), bf16),
            pltpu.VMEM((768, 1152), bf16),
            pltpu.VMEM((2304, 1152), bf16),
            pltpu.VMEM((CHUNK, 1152), f32),
            pltpu.VMEM((192, 1152), bf16),
            pltpu.VMEM((192, 768), bf16),
            pltpu.VMEM((2, RANK, 1152), f32),
            pltpu.VMEM((RANK, 1152), f32),
            pltpu.VMEM((RANK, 1152), f32),
            pltpu.VMEM((NZ, 8, 1152), f32),
            pltpu.VMEM((2, RANK, 1152), f32),
            pltpu.VMEM((192, 2304), bf16),
            pltpu.VMEM((RANK, 1152), f32),
            pltpu.VMEM((RANK, 640), f32),
            pltpu.VMEM((RANK, 640), f32),
            pltpu.VMEM((NZ, 8, 640), f32),
            pltpu.VMEM((RANK, 1152), f32),
            pltpu.VMEM((RANK, 128), f32),
            pltpu.VMEM((2304, 1152), bf16),
            pltpu.VMEM((2, 2304, TILE), f32),
            pltpu.VMEM((2, 2, 4, CHUNK, TILE), f32),
            pltpu.VMEM((2, 2, 4, HALF, TILE), f32),
            pltpu.VMEM((2, 2, 1, CHUNK, TILE), f32),
            pltpu.VMEM((2, 2, 1, HALF, TILE), f32),
            dma((5,)),
            dma((8,)),
        ]
        + [dma((NZ,))] * 8
        + [
            dma((2, 5)),
            dma((2, 5)),
            dma((2, 5)),
            dma((2, 5)),
            dma((2, NDP, 2)),
            dma((2, 2, 4, 2)),
            dma((2, 2, 4)),
            dma((2, NDP, 2)),
            dma((2, 2, 1, 2)),
            dma((2, 2, 1)),
        ],
        compiler_params=pltpu.CompilerParams(
            collective_id=0, has_side_effects=True, vmem_limit_bytes=56 * 2**20
        ),
        cost_estimate=pl.CostEstimate(
            flops=8 * 10**9, bytes_accessed=14 * 10**6, transcendentals=0
        ),
        name="fused",
    )(tokens, cot, weight, carried, momentum, q_t)


def body(tokens, up_cotangent, up_weight, carried, momentum, q_start):
    feature_t, right_t, new_momentum = fused(
        tokens, up_cotangent, up_weight, carried[0], momentum, q_start.T
    )
    return (feature_t.T, right_t.T, new_momentum)


def solution(mesh):
    placed = (
        P("dp", None),
        P("dp", "mp"),
        P("dp", "mp"),
        P("dp", None, "mp"),
        P("dp", "mp"),
        P("mp", None),
    )
    return jax.shard_map(
        body,
        mesh=mesh,
        in_specs=placed,
        out_specs=(P("dp", "mp"), P("mp", None), P("dp", "mp")),
        check_vma=False,
    )
```

```python
import jax
import jax.numpy as jnp
from jax import lax
from jax.experimental import pallas as pl
from jax.experimental.pallas import tpu as pltpu
from jax.sharding import PartitionSpec as P

DECAY = 0.9
MESH = pl.DeviceIdType.MESH
NT = (((1,), (1,)), ((), ()))
NN = (((1,), (0,)), ((), ()))
TN = (((0,), (0,)), ((), ()))
NZ = 8
NDP = 16
RANK = 64
TILE = 384
FAR_FIRST = (4, 3, 5, 2, 6, 1, 7)
NEAR_FIRST = (1, 7, 2, 6, 3, 5, 4)
CHUNK = 144
HALF = 72
SPLIT = 80


def mm(a, b, dims):
    return lax.dot_general(a, b, dims, preferred_element_type=jnp.float32)


def mm32(a, b, dims):
    return lax.dot_general(
        a, b, dims, precision=lax.Precision.HIGHEST, preferred_element_type=jnp.float32
    )


def split3(x):
    hi = x.astype(jnp.bfloat16)
    rest = x - hi.astype(jnp.float32)
    mid = rest.astype(jnp.bfloat16)
    low = (rest - mid.astype(jnp.float32)).astype(jnp.bfloat16)
    return jnp.concatenate([hi, mid, low], axis=0)


def fold3(x):
    return x[0:RANK] + x[RANK : 2 * RANK] + x[2 * RANK :]


def aligned(i, n):
    return pl.multiple_of(i * n, n)


def fused_kernel(
    tokens_hbm, cot_hbm, weight_hbm, carried_hbm, momentum_hbm, q_ref,
    feature_ref, right_ref, mom_ref,
    tokens, cot, carried, momentum, q3, t3, lp, sib_l, cs, rsl, left, left3,
    yp, sib_y, ys, rsy, yf, elim,
    weight, part, r1, rl1, r2, rl2,
    load_sem, sib_sem, rs_s, rs_r, ag_s, ag_r, yrs_s, yrs_r, yag_s, yag_r,
    fw_s, fw_r, yfw_s, yfw_r,
    w_s, w_r, ws_s, ws_r, f1_s, r1_r, rl1_r, f2_s, r2_r, rl2_r,
):
    dp = lax.axis_index("dp")
    mp = lax.axis_index("mp")
    z, c = dp // 2, dp % 2
    x, y = mp // 4, mp % 4
    sib = (z * 2 + 1 - c, mp)

    def zdev(d):
        return ((z + d) % NZ * 2 + c, mp)

    def xydev(axis, d):
        if axis == 0:
            return (dp, (x + d) % 4 * 4 + y)
        return (dp, x * 4 + (y + d) % 4)

    def remote(src, dst, send, recv, device):
        return pltpu.make_async_remote_copy(
            src_ref=src, dst_ref=dst, send_sem=send, recv_sem=recv,
            device_id=device, device_id_type=MESH,
        )

    own_chunk = pl.ds(pl.multiple_of(dp * CHUNK, 16), CHUNK)
    loads = [
        pltpu.make_async_copy(src, dst, load_sem.at[i])
        for i, (src, dst) in enumerate(
            (
                (weight_hbm, weight.at[own_chunk, :]), (cot_hbm, cot), (tokens_hbm, tokens),
                (carried_hbm, carried), (momentum_hbm, momentum),
            )
        )
    ]
    for copy in loads:
        copy.start()
    barrier = pltpu.get_barrier_semaphore()
    pl.semaphore_signal(barrier, inc=1, device_id=sib, device_id_type=MESH)
    for d in FAR_FIRST:
        pl.semaphore_signal(barrier, inc=1, device_id=zdev(d), device_id_type=MESH)
    for axis in range(2):
        for d in (1, 3):
            pl.semaphore_signal(barrier, inc=1, device_id=xydev(axis, d), device_id_type=MESH)

    def weight_rows(way, s, core, first=0, count=CHUNK):
        place = (z - s + NZ) % NZ if way == 0 else (z + s) % NZ
        return weight.at[pl.ds(pl.multiple_of((place * 2 + core) * CHUNK + first, 16), count), :]

    def ring_copy(way, s):
        first, count = 0, CHUNK
        if s == 4:
            first, count = (0, SPLIT) if way == 0 else (SPLIT, CHUNK - SPLIT)
        src = weight_rows(way, s - 1, c, first, count)
        return remote(src, src, w_s.at[way, s - 1], w_r.at[way, s], zdev(1 if way == 0 else NZ - 1))

    def ring_arrival(way, s):
        first, count = 0, CHUNK
        if s == 4:
            first, count = (0, SPLIT) if way == 0 else (SPLIT, CHUNK - SPLIT)
        dst = weight_rows(way, s, c, first, count)
        return remote(dst, dst, w_s.at[way, s - 1], w_r.at[way, s], zdev(1))

    def pair_copy(way, s, core):
        rows = weight_rows(way, s, core)
        return remote(rows, rows, ws_s.at[way, s], ws_r.at[way, s], sib)

    def ways_of(s):
        return (0,) if s in (0, 4) else (0, 1)

    def ring_step(s):
        for way in (0, 1):
            if s > 0:
                ring_arrival(way, s).wait_recv()
            if s < 4:
                ring_copy(way, s + 1).start()
            if s in (1, 2, 3):
                pair_copy(way, s, c).start()
        if s in (0, 4):
            pair_copy(0, s, c).start()

    def block(h, j, upper):
        return part.at[h, pl.ds(pl.multiple_of(j * CHUNK + (0 if upper else HALF), 8), HALF), :]

    def rows_of(upper):
        return pl.ds(0 if upper else HALF, HALF)

    class Stage:
        def __init__(self, number):
            self.number = number
            self.sends, self.arrive, self.passed = ((f1_s, r1_r, rl1_r), (f2_s, r2_r, rl2_r))[number]
            self.into, self.relay = ((r1, rl1), (r2, rl2))[number]

        def axis(self, h):
            return h if self.number == 0 else 1 - h

        def slot(self, h, j):
            if self.number == 1:
                return 0
            return j % 4 if h == 0 else j // 4

        def distance(self, h, j):
            if self.axis(h) == 0:
                return (j // 4 - x + 4) % 4
            return (j % 4 - y + 4) % 4

        def send(self, h, j, upper, direct, way):
            k = self.slot(h, j)
            source = block(h, j, upper)
            part_id = 0 if upper else 1
            if direct:
                dst = self.into.at[h, way, k, rows_of(upper), :]
                recv = self.arrive.at[h, way, k, part_id]
            else:
                dst = self.relay.at[h, way, k]
                recv = self.passed.at[h, way, k]
            return remote(
                source, dst, self.sends.at[h, j, part_id], recv,
                xydev(self.axis(h), 1 if way == 0 else 3),
            )

        def far(self, h, j):
            @pl.when(self.distance(h, j) == 2)
            def _():
                self.send(h, j, True, False, 0).start()
                self.send(h, j, False, False, 1).start()

        def near(self, h, j):
            far = self.distance(h, j)

            @pl.when(far == 1)
            def _():
                self.send(h, j, False, True, 0).start()

            @pl.when(far == 3)
            def _():
                self.send(h, j, True, True, 1).start()

        def merge(self, h, j):
            far = self.distance(h, j)
            k = self.slot(h, j)

            def one(way, upper):
                rows = block(h, j, upper)
                copy = remote(
                    self.relay.at[h, way, k], self.relay.at[h, way, k],
                    self.sends.at[h, j, 0], self.passed.at[h, way, k], xydev(self.axis(h), 1),
                )
                copy.wait_recv()
                rows[...] = rows[...] + self.relay[h, way, k]
                self.send(h, j, upper, True, way).start()

            @pl.when(far == 1)
            def _():
                one(0, True)

            @pl.when(far == 3)
            def _():
                one(1, False)

        def collect(self, h, j):
            k = self.slot(h, j)
            for way in range(2):
                for upper in (True, False):
                    dst = self.into.at[h, way, k, rows_of(upper), :]
                    remote(
                        dst, dst, self.sends.at[h, j, 0],
                        self.arrive.at[h, way, k, 0 if upper else 1], xydev(self.axis(h), 1),
                    ).wait_recv()
            own = pl.ds(pl.multiple_of(j * CHUNK, 8), CHUNK)
            return part[h, own, :] + self.into[h, 0, k] + self.into[h, 1, k]

        def drain(self, h, j):
            @pl.when(self.distance(h, j) != 0)
            def _():
                for upper in (True, False):
                    self.send(h, j, upper, True, 0).wait_send()

    first, second = Stage(0), Stage(1)

    def place_of(way, s):
        return (z - s + NZ) % NZ if way == 0 else (z + s) % NZ

    def units_of(s):
        for way in ways_of(s):
            for b in range(2):
                for h in range(2):
                    yield h, place_of(way, s) * 2 + b

    def partials(s):
        for way in ways_of(s):
            pair_copy(way, s, 1 - c).wait_recv()
            rows = pl.ds(pl.multiple_of(place_of(way, s) * (2 * CHUNK), 16), 2 * CHUNK)
            for h in range(2):
                part[h, rows, :] = mm(weight[rows, :], cot[pl.ds(h * TILE, TILE), :], NT)
        for h, j in units_of(s):
            first.far(h, j)
        for h, j in units_of(s):
            first.near(h, j)

    def merges(s):
        for h, j in units_of(s):
            first.merge(h, j)

    def completes(s):
        for h, j in units_of(s):

            @pl.when(first.distance(h, j) == 0)
            def _(h=h, j=j):
                part[h, pl.ds(pl.multiple_of(j * CHUNK, 8), CHUNK), :] = first.collect(h, j)
                second.far(h, j)
                second.near(h, j)

    def second_merges(s):
        for h, j in units_of(s):

            @pl.when(first.distance(h, j) == 0)
            def _(h=h, j=j):
                second.merge(h, j)

    def own_block(h, k):
        return x * 4 + k if h == 0 else k * 4 + y

    def feature_finish():
        for h in range(2):
            feature_ref[:, pl.ds(h * TILE, TILE)] = second.collect(h, mp)

    q3[...] = split3(q_ref[...])
    loads[1].wait()
    for t in range(2):
        rows = pl.ds(t * TILE, TILE)
        t3[:, rows] = split3(fold3(mm(q3[...], cot[rows, :], NT)))
    loads[0].wait()
    pl.semaphore_wait(barrier, NZ + 4)
    ring_step(0)

    loads[2].wait()
    loads[3].wait()

    def left_half(h):
        def tile(t, _):
            columns = pl.ds(aligned(h * 3 + t, TILE), TILE)
            value = mm(q3[...], carried[columns, :], NT) + mm(t3[...], tokens[:, columns], NN)
            lp[h, :, pl.ds(aligned(t, TILE), TILE)] = fold3(value)
            return 0

        lax.fori_loop(0, 3, tile, 0)

    def exchange(src, dst, slot):
        return remote(src, dst, sib_sem.at[2 * slot], sib_sem.at[2 * slot + 1], sib)

    def scatter(src, dst, send, recv):
        copies = []
        for d in FAR_FIRST:
            copy = remote(
                src.at[pl.ds(aligned((z + d) % NZ, 8), 8), :], dst.at[d],
                send.at[d], recv.at[d], zdev(d),
            )
            copy.start()
            copies.append(copy)
        return copies

    def gather(block_of, send, recv, given_of, pass_send, pass_recv):
        copies = []
        for d in FAR_FIRST:
            copy = remote(block_of(z), block_of(z), send.at[d], recv.at[d], zdev(d))
            copy.start()
            copies.append(copy)

        def give(d):
            rows = given_of((z - d + NZ) % NZ, c)
            copy = remote(rows, rows, pass_send.at[d], pass_recv.at[d], sib)
            copy.start()
            copies.append(copy)

        give(0)

        def finish():
            for d in NEAR_FIRST:
                rows = block_of((z - d + NZ) % NZ)
                remote(rows, rows, send.at[d], recv.at[d], zdev(d)).wait_recv()
                give(d)

        def taken():
            for d in (0,) + NEAR_FIRST:
                rows = given_of((z - d + NZ) % NZ, 1 - c)
                remote(rows, rows, pass_send.at[d], pass_recv.at[d], sib).wait_recv()

        def sent():
            for copy in copies:
                copy.wait_send()

        return finish, taken, sent

    left_half(1 - c)
    pair = exchange(lp.at[1 - c], sib_l, 0)
    pair.start()
    left_half(c)
    partials(0)
    ring_step(1)
    partials(1)
    pair.wait()
    cs[...] = lp[c] + sib_l[...]
    ring_step(2)
    copies = scatter(cs, rsl, rs_s, rs_r)
    merges(0)
    partials(2)
    merges(1)
    completes(0)
    ring_step(3)
    partials(3)
    own_rows = pl.ds(aligned(z, 8), 8)
    total = cs[own_rows, :]
    for copy in copies:
        copy.wait_recv()
    for d in range(1, NZ):
        total = total + rsl[d]
    left[c, own_rows, :] = total * (1.0 / NDP)

    def left_block(j, core):
        return left.at[core, pl.ds(aligned(j, 8), 8), :]

    finish, taken, sent = gather(
        lambda j: left_block(j, c), ag_s, ag_r, left_block, fw_s, fw_r
    )
    ring_step(4)
    partials(4)
    merges(2)
    completes(1)
    finish()

    def half_columns(h):
        return pl.ds(aligned(h, 1152), 1152)

    left3[:, half_columns(c)] = split3(left[c])
    t2 = []
    for t in range(2):
        t2.append(
            mm(left3[:, half_columns(c)], tokens[pl.ds(t * TILE, TILE), half_columns(c)], NT)
        )
    taken()
    left3[:, half_columns(1 - c)] = split3(left[1 - c])
    for t in range(2):
        rows = pl.ds(t * TILE, TILE)
        rest = mm(left3[:, half_columns(1 - c)], tokens[rows, half_columns(1 - c)], NT)
        t3[:, rows] = split3(fold3(t2[t] + rest))

    def y_tile(t):
        columns = pl.ds(aligned(t, TILE), TILE)
        value = mm(left3[...], carried[:, columns], NN) + mm(t3[...], cot[:, columns], NN)
        yp[:, columns] = fold3(value)

    def y_first(i, _):
        y_tile(c * i + (1 - c) * (2 - i))
        return 0

    def mine(core):
        return pl.ds(pl.multiple_of(core * 512, 128), 640)

    lax.fori_loop(0, 2, y_first, 0)
    pair = exchange(yp.at[:, mine(1 - c)], sib_y, 1)
    pair.start()
    y_tile(2 * c)
    pair.wait()
    ys[...] = yp[:, mine(c)] + sib_y[...]
    copies += scatter(ys, rsy, yrs_s, yrs_r)
    merges(3)
    completes(2)
    second_merges(0)
    merges(4)
    second_merges(1)

    products = mm(left3[...], left3[...], NT)
    gram = jnp.zeros((RANK, RANK), jnp.float32)
    for i in (2, 1, 0):
        for j in (2, 1, 0):
            gram = gram + products[i * RANK : (i + 1) * RANK, j * RANK : (j + 1) * RANK]
    row_id = lax.broadcasted_iota(jnp.int32, (RANK, 2 * RANK), 0)
    lane_id = lax.broadcasted_iota(jnp.int32, (RANK, 2 * RANK), 1)
    elim[:, 0:RANK] = gram
    elim[:, RANK:] = jnp.where(row_id[:, 0:RANK] == lane_id[:, 0:RANK], 1.0, 0.0)

    def eliminate(j, _):
        row = elim[pl.ds(j, 1), :]
        full = elim[...]
        pivot = jnp.sum(jnp.where(lane_id[0:1] == j, row, 0.0), axis=1, keepdims=True)
        column = jnp.sum(jnp.where(lane_id == j, full, 0.0), axis=1, keepdims=True)
        factor = jnp.where(row_id[:, 0:1] > j, column / pivot, 0.0)
        elim[...] = full - factor * row
        return 0

    lax.fori_loop(0, RANK - 1, eliminate, 0)

    total = ys[own_rows, :]
    for copy in copies[7:]:
        copy.wait_recv()
    for d in range(1, NZ):
        total = total + rsy[d]
    yf[own_rows, mine(c)] = total

    def y_given(j, core):
        return yf.at[pl.ds(aligned(j, 8), 8), pl.ds(pl.multiple_of(core * 640, 128), 512)]

    y_finish, y_taken, y_sent = gather(
        lambda j: yf.at[pl.ds(aligned(j, 8), 8), mine(c)], yag_s, yag_r, y_given, yfw_s, yfw_r
    )
    done = elim[...]
    diagonal = jnp.sum(jnp.where(lane_id == row_id, done, 0.0), axis=1, keepdims=True)
    inverse = done[:, RANK:] / jnp.sqrt(diagonal)
    k = dp % 8
    window = left[dp // 8, :, pl.ds(aligned(k, 128), 256)]
    own_left = pltpu.roll(window, (256 - 16 * k) % 256, 1)[:, 0:CHUNK]
    own_basis = mm32(inverse, own_left, NN)
    completes(3)
    second_merges(2)
    y_finish()
    completes(4)
    second_merges(3)
    y_taken()
    loads[4].wait()
    for t in range(3):
        columns = pl.ds(t * TILE, TILE)
        right = mm32(inverse, yf[:, columns], NN) * (1.0 / NDP)
        right_ref[:, columns] = right
        mom_ref[:, columns] = DECAY * momentum[:, columns] + mm32(own_basis, right, TN)
    second_merges(4)
    feature_finish()

    for copy in copies:
        copy.wait_send()
    sent()
    y_sent()
    for s in range(5):
        for way in (0, 1):
            if s < 4:
                ring_copy(way, s + 1).wait_send()
            if way in ways_of(s):
                pair_copy(way, s, c).wait_send()

    def drain(j, _):
        for h in range(2):
            first.drain(h, j)
        return 0

    lax.fori_loop(0, NDP, drain, 0)

    def drain_second(k, _):
        for h in range(2):
            second.drain(h, own_block(h, k))
        return 0

    lax.fori_loop(0, 4, drain_second, 0)


def fused(tokens, cot, weight, carried, momentum, q_t):
    f32, bf16 = jnp.float32, jnp.bfloat16
    dma = pltpu.SemaphoreType.DMA
    hbm = pl.BlockSpec(memory_space=pl.ANY)
    vmem = pl.BlockSpec(memory_space=pltpu.VMEM)
    return pl.pallas_call(
        fused_kernel,
        out_shape=(
            jax.ShapeDtypeStruct((CHUNK, 768), f32),
            jax.ShapeDtypeStruct((RANK, 1152), f32),
            jax.ShapeDtypeStruct((CHUNK, 1152), f32),
        ),
        in_specs=[hbm] * 5 + [vmem],
        out_specs=(vmem, vmem, vmem),
        scratch_shapes=[
            pltpu.VMEM((768, 2304), bf16),
            pltpu.VMEM((768, 1152), bf16),
            pltpu.VMEM((2304, 1152), bf16),
            pltpu.VMEM((CHUNK, 1152), f32),
            pltpu.VMEM((192, 1152), bf16),
            pltpu.VMEM((192, 768), bf16),
            pltpu.VMEM((2, RANK, 1152), f32),
            pltpu.VMEM((RANK, 1152), f32),
            pltpu.VMEM((RANK, 1152), f32),
            pltpu.VMEM((NZ, 8, 1152), f32),
            pltpu.VMEM((2, RANK, 1152), f32),
            pltpu.VMEM((192, 2304), bf16),
            pltpu.VMEM((RANK, 1152), f32),
            pltpu.VMEM((RANK, 640), f32),
            pltpu.VMEM((RANK, 640), f32),
            pltpu.VMEM((NZ, 8, 640), f32),
            pltpu.VMEM((RANK, 1152), f32),
            pltpu.VMEM((RANK, 128), f32),
            pltpu.VMEM((2304, 1152), bf16),
            pltpu.VMEM((2, 2304, TILE), f32),
            pltpu.VMEM((2, 2, 4, CHUNK, TILE), f32),
            pltpu.VMEM((2, 2, 4, HALF, TILE), f32),
            pltpu.VMEM((2, 2, 1, CHUNK, TILE), f32),
            pltpu.VMEM((2, 2, 1, HALF, TILE), f32),
            dma((5,)),
            dma((4,)),
        ]
        + [dma((NZ,))] * 12
        + [
            dma((2, 5)),
            dma((2, 5)),
            dma((2, 5)),
            dma((2, 5)),
            dma((2, NDP, 2)),
            dma((2, 2, 4, 2)),
            dma((2, 2, 4)),
            dma((2, NDP, 2)),
            dma((2, 2, 1, 2)),
            dma((2, 2, 1)),
        ],
        compiler_params=pltpu.CompilerParams(
            collective_id=0, has_side_effects=True, vmem_limit_bytes=56 * 2**20
        ),
        cost_estimate=pl.CostEstimate(
            flops=8 * 10**9, bytes_accessed=14 * 10**6, transcendentals=0
        ),
        name="fused",
    )(tokens, cot, weight, carried, momentum, q_t)


def hand_on_kernel(*refs):
    sources, results, held, sems = refs[0:3], refs[3:6], refs[6:9], refs[9]
    loads = [pltpu.make_async_copy(sources[i], held[i], sems.at[i]) for i in range(3)]
    stores = [pltpu.make_async_copy(held[i], results[i], sems.at[3 + i]) for i in range(3)]
    for copy in loads:
        copy.start()
    for load, store in zip(loads, stores):
        load.wait()
        store.start()
    for copy in stores:
        copy.wait()


def hand_on(*arrays):
    hbm = pl.BlockSpec(memory_space=pl.ANY)
    return pl.pallas_call(
        hand_on_kernel,
        out_shape=tuple(jax.ShapeDtypeStruct(a.shape, a.dtype) for a in arrays),
        in_specs=[hbm] * 3,
        out_specs=(hbm,) * 3,
        scratch_shapes=[pltpu.VMEM(a.shape, a.dtype) for a in arrays]
        + [pltpu.SemaphoreType.DMA((6,))],
        name="hand_on",
    )(*arrays)


def body(tokens, up_cotangent, up_weight, carried, momentum, q_start):
    feature_t, right_t, new_momentum = fused(
        tokens, up_cotangent, up_weight, carried[0], momentum, q_start.T
    )
    feature_t, right_t, new_momentum = hand_on(feature_t, right_t, new_momentum)
    return (feature_t.T, right_t.T, new_momentum)


def solution(mesh):
    placed = (
        P("dp", None),
        P("dp", "mp"),
        P("dp", "mp"),
        P("dp", None, "mp"),
        P("dp", "mp"),
        P("mp", None),
    )
    return jax.shard_map(
        body,
        mesh=mesh,
        in_specs=placed,
        out_specs=(P("dp", "mp"), P("mp", None), P("dp", "mp")),
        check_vma=False,
    )
```

```python
import jax
import jax.numpy as jnp
from jax import lax
from jax.experimental import pallas as pl
from jax.experimental.pallas import tpu as pltpu
from jax.sharding import PartitionSpec as P

DECAY = 0.9
MESH = pl.DeviceIdType.MESH
NT = (((1,), (1,)), ((), ()))
NN = (((1,), (0,)), ((), ()))
TN = (((0,), (0,)), ((), ()))
NZ = 8
NDP = 16
RANK = 64
TILE = 384
FAR_FIRST = (4, 3, 5, 2, 6, 1, 7)
NEAR_FIRST = (1, 7, 2, 6, 3, 5, 4)
CHUNK = 144
HALF = 72
SPLIT = 80


def mm(a, b, dims):
    return lax.dot_general(a, b, dims, preferred_element_type=jnp.float32)


def mm32(a, b, dims):
    return lax.dot_general(
        a, b, dims, precision=lax.Precision.HIGHEST, preferred_element_type=jnp.float32
    )


def split3(x):
    hi = x.astype(jnp.bfloat16)
    rest = x - hi.astype(jnp.float32)
    mid = rest.astype(jnp.bfloat16)
    low = (rest - mid.astype(jnp.float32)).astype(jnp.bfloat16)
    return jnp.concatenate([hi, mid, low], axis=0)


def fold3(x):
    return x[0:RANK] + x[RANK : 2 * RANK] + x[2 * RANK :]


def aligned(i, n):
    return pl.multiple_of(i * n, n)


def fused_kernel(
    tokens_hbm, cot_hbm, weight_hbm, carried_hbm, momentum_hbm, q_ref,
    feature_ref, right_ref, mom_ref,
    tokens, cot, carried, momentum, q3, t3, lp, sib_l, cs, rsl, left, left3,
    yp, sib_y, ys, rsy, yf, elim,
    weight, part, r1, rl1, r2, rl2,
    load_sem, sib_sem, rs_s, rs_r, ag_s, ag_r, yrs_s, yrs_r, yag_s, yag_r,
    fw_s, fw_r, yfw_s, yfw_r,
    w_s, w_r, ws_s, ws_r, f1_s, r1_r, rl1_r, f2_s, r2_r, rl2_r,
):
    dp = lax.axis_index("dp")
    mp = lax.axis_index("mp")
    z, c = dp // 2, dp % 2
    x, y = mp // 4, mp % 4
    sib = (z * 2 + 1 - c, mp)

    def zdev(d):
        return ((z + d) % NZ * 2 + c, mp)

    def xydev(axis, d):
        if axis == 0:
            return (dp, (x + d) % 4 * 4 + y)
        return (dp, x * 4 + (y + d) % 4)

    def remote(src, dst, send, recv, device):
        return pltpu.make_async_remote_copy(
            src_ref=src, dst_ref=dst, send_sem=send, recv_sem=recv,
            device_id=device, device_id_type=MESH,
        )

    own_chunk = pl.ds(pl.multiple_of(dp * CHUNK, 16), CHUNK)
    loads = [
        pltpu.make_async_copy(src, dst, load_sem.at[i])
        for i, (src, dst) in enumerate(
            (
                (weight_hbm, weight.at[own_chunk, :]), (cot_hbm, cot), (tokens_hbm, tokens),
                (carried_hbm, carried), (momentum_hbm, momentum),
            )
        )
    ]
    for copy in loads:
        copy.start()
    barrier = pltpu.get_barrier_semaphore()
    pl.semaphore_signal(barrier, inc=1, device_id=sib, device_id_type=MESH)
    for d in FAR_FIRST:
        pl.semaphore_signal(barrier, inc=1, device_id=zdev(d), device_id_type=MESH)
    for axis in range(2):
        for d in (1, 3):
            pl.semaphore_signal(barrier, inc=1, device_id=xydev(axis, d), device_id_type=MESH)

    def weight_rows(way, s, core, first=0, count=CHUNK):
        place = (z - s + NZ) % NZ if way == 0 else (z + s) % NZ
        return weight.at[pl.ds(pl.multiple_of((place * 2 + core) * CHUNK + first, 16), count), :]

    def ring_copy(way, s):
        first, count = 0, CHUNK
        if s == 4:
            first, count = (0, SPLIT) if way == 0 else (SPLIT, CHUNK - SPLIT)
        src = weight_rows(way, s - 1, c, first, count)
        return remote(src, src, w_s.at[way, s - 1], w_r.at[way, s], zdev(1 if way == 0 else NZ - 1))

    def ring_arrival(way, s):
        first, count = 0, CHUNK
        if s == 4:
            first, count = (0, SPLIT) if way == 0 else (SPLIT, CHUNK - SPLIT)
        dst = weight_rows(way, s, c, first, count)
        return remote(dst, dst, w_s.at[way, s - 1], w_r.at[way, s], zdev(1))

    def pair_copy(way, s, core):
        rows = weight_rows(way, s, core)
        return remote(rows, rows, ws_s.at[way, s], ws_r.at[way, s], sib)

    def ways_of(s):
        return (0,) if s in (0, 4) else (0, 1)

    def ring_step(s):
        for way in (0, 1):
            if s > 0:
                ring_arrival(way, s).wait_recv()
            if s < 4:
                ring_copy(way, s + 1).start()
            if s in (1, 2, 3):
                pair_copy(way, s, c).start()
        if s in (0, 4):
            pair_copy(0, s, c).start()

    def block(h, j, upper):
        return part.at[h, pl.ds(pl.multiple_of(j * CHUNK + (0 if upper else HALF), 8), HALF), :]

    def rows_of(upper):
        return pl.ds(0 if upper else HALF, HALF)

    class Stage:
        def __init__(self, number):
            self.number = number
            self.sends, self.arrive, self.passed = ((f1_s, r1_r, rl1_r), (f2_s, r2_r, rl2_r))[number]
            self.into, self.relay = ((r1, rl1), (r2, rl2))[number]

        def axis(self, h):
            return h if self.number == 0 else 1 - h

        def slot(self, h, j):
            if self.number == 1:
                return 0
            return j % 4 if h == 0 else j // 4

        def distance(self, h, j):
            if self.axis(h) == 0:
                return (j // 4 - x + 4) % 4
            return (j % 4 - y + 4) % 4

        def send(self, h, j, upper, direct, way):
            k = self.slot(h, j)
            source = block(h, j, upper)
            part_id = 0 if upper else 1
            if direct:
                dst = self.into.at[h, way, k, rows_of(upper), :]
                recv = self.arrive.at[h, way, k, part_id]
            else:
                dst = self.relay.at[h, way, k]
                recv = self.passed.at[h, way, k]
            return remote(
                source, dst, self.sends.at[h, j, part_id], recv,
                xydev(self.axis(h), 1 if way == 0 else 3),
            )

        def far(self, h, j):
            @pl.when(self.distance(h, j) == 2)
            def _():
                self.send(h, j, True, False, 0).start()
                self.send(h, j, False, False, 1).start()

        def near(self, h, j):
            far = self.distance(h, j)

            @pl.when(far == 1)
            def _():
                self.send(h, j, False, True, 0).start()

            @pl.when(far == 3)
            def _():
                self.send(h, j, True, True, 1).start()

        def merge(self, h, j):
            far = self.distance(h, j)
            k = self.slot(h, j)

            def one(way, upper):
                rows = block(h, j, upper)
                copy = remote(
                    self.relay.at[h, way, k], self.relay.at[h, way, k],
                    self.sends.at[h, j, 0], self.passed.at[h, way, k], xydev(self.axis(h), 1),
                )
                copy.wait_recv()
                rows[...] = rows[...] + self.relay[h, way, k]
                self.send(h, j, upper, True, way).start()

            @pl.when(far == 1)
            def _():
                one(0, True)

            @pl.when(far == 3)
            def _():
                one(1, False)

        def collect(self, h, j):
            k = self.slot(h, j)
            for way in range(2):
                for upper in (True, False):
                    dst = self.into.at[h, way, k, rows_of(upper), :]
                    remote(
                        dst, dst, self.sends.at[h, j, 0],
                        self.arrive.at[h, way, k, 0 if upper else 1], xydev(self.axis(h), 1),
                    ).wait_recv()
            own = pl.ds(pl.multiple_of(j * CHUNK, 8), CHUNK)
            return part[h, own, :] + self.into[h, 0, k] + self.into[h, 1, k]

        def drain(self, h, j):
            @pl.when(self.distance(h, j) != 0)
            def _():
                for upper in (True, False):
                    self.send(h, j, upper, True, 0).wait_send()

    first, second = Stage(0), Stage(1)

    def place_of(way, s):
        return (z - s + NZ) % NZ if way == 0 else (z + s) % NZ

    def units_of(s):
        for way in ways_of(s):
            for b in range(2):
                for h in range(2):
                    yield h, place_of(way, s) * 2 + b

    def partials(s):
        for way in ways_of(s):
            pair_copy(way, s, 1 - c).wait_recv()
            rows = pl.ds(pl.multiple_of(place_of(way, s) * (2 * CHUNK), 16), 2 * CHUNK)
            for h in range(2):
                part[h, rows, :] = mm(weight[rows, :], cot[pl.ds(h * TILE, TILE), :], NT)
        for h, j in units_of(s):
            first.far(h, j)
        for h, j in units_of(s):
            first.near(h, j)

    def merges(s):
        for h, j in units_of(s):
            first.merge(h, j)

    def completes(s):
        for h, j in units_of(s):

            @pl.when(first.distance(h, j) == 0)
            def _(h=h, j=j):
                part[h, pl.ds(pl.multiple_of(j * CHUNK, 8), CHUNK), :] = first.collect(h, j)
                second.far(h, j)
                second.near(h, j)

    def second_merges(s):
        for h, j in units_of(s):

            @pl.when(first.distance(h, j) == 0)
            def _(h=h, j=j):
                second.merge(h, j)

    def own_block(h, k):
        return x * 4 + k if h == 0 else k * 4 + y

    def feature_finish():
        for h in range(2):
            feature_ref[:, pl.ds(h * TILE, TILE)] = second.collect(h, mp)

    loads[0].wait()
    pl.semaphore_wait(barrier, NZ + 4)
    ring_step(0)
    loads[1].wait()
    partials(0)
    q3[...] = split3(q_ref[...])
    for t in range(2):
        rows = pl.ds(t * TILE, TILE)
        t3[:, rows] = split3(fold3(mm(q3[...], cot[rows, :], NT)))

    loads[2].wait()
    loads[3].wait()

    def left_half(h):
        def tile(t, _):
            columns = pl.ds(aligned(h * 3 + t, TILE), TILE)
            value = mm(q3[...], carried[columns, :], NT) + mm(t3[...], tokens[:, columns], NN)
            lp[h, :, pl.ds(aligned(t, TILE), TILE)] = fold3(value)
            return 0

        lax.fori_loop(0, 3, tile, 0)

    def exchange(src, dst, slot):
        return remote(src, dst, sib_sem.at[2 * slot], sib_sem.at[2 * slot + 1], sib)

    def scatter(src, dst, send, recv):
        copies = []
        for d in FAR_FIRST:
            copy = remote(
                src.at[pl.ds(aligned((z + d) % NZ, 8), 8), :], dst.at[d],
                send.at[d], recv.at[d], zdev(d),
            )
            copy.start()
            copies.append(copy)
        return copies

    def gather(block_of, send, recv, given_of, pass_send, pass_recv):
        copies = []
        for d in FAR_FIRST:
            copy = remote(block_of(z), block_of(z), send.at[d], recv.at[d], zdev(d))
            copy.start()
            copies.append(copy)

        def give(d):
            rows = given_of((z - d + NZ) % NZ, c)
            copy = remote(rows, rows, pass_send.at[d], pass_recv.at[d], sib)
            copy.start()
            copies.append(copy)

        give(0)

        def finish():
            for d in NEAR_FIRST:
                rows = block_of((z - d + NZ) % NZ)
                remote(rows, rows, send.at[d], recv.at[d], zdev(d)).wait_recv()
                give(d)

        def taken():
            for d in (0,) + NEAR_FIRST:
                rows = given_of((z - d + NZ) % NZ, 1 - c)
                remote(rows, rows, pass_send.at[d], pass_recv.at[d], sib).wait_recv()

        def sent():
            for copy in copies:
                copy.wait_send()

        return finish, taken, sent

    left_half(1 - c)
    pair = exchange(lp.at[1 - c], sib_l, 0)
    pair.start()
    ring_step(1)
    partials(1)
    left_half(c)
    pair.wait()
    cs[...] = lp[c] + sib_l[...]
    ring_step(2)
    partials(2)
    ring_step(3)
    copies = scatter(cs, rsl, rs_s, rs_r)
    merges(0)
    partials(3)
    merges(1)
    ring_step(4)
    partials(4)
    own_rows = pl.ds(aligned(z, 8), 8)
    total = cs[own_rows, :]
    for copy in copies:
        copy.wait_recv()
    for d in range(1, NZ):
        total = total + rsl[d]
    left[c, own_rows, :] = total * (1.0 / NDP)

    def left_block(j, core):
        return left.at[core, pl.ds(aligned(j, 8), 8), :]

    finish, taken, sent = gather(
        lambda j: left_block(j, c), ag_s, ag_r, left_block, fw_s, fw_r
    )
    merges(2)
    completes(0)
    finish()

    def half_columns(h):
        return pl.ds(aligned(h, 1152), 1152)

    left3[:, half_columns(c)] = split3(left[c])
    t2 = []
    for t in range(2):
        t2.append(
            mm(left3[:, half_columns(c)], tokens[pl.ds(t * TILE, TILE), half_columns(c)], NT)
        )
    taken()
    left3[:, half_columns(1 - c)] = split3(left[1 - c])
    for t in range(2):
        rows = pl.ds(t * TILE, TILE)
        rest = mm(left3[:, half_columns(1 - c)], tokens[rows, half_columns(1 - c)], NT)
        t3[:, rows] = split3(fold3(t2[t] + rest))

    def y_tile(t):
        columns = pl.ds(aligned(t, TILE), TILE)
        value = mm(left3[...], carried[:, columns], NN) + mm(t3[...], cot[:, columns], NN)
        yp[:, columns] = fold3(value)

    def y_first(i, _):
        y_tile(c * i + (1 - c) * (2 - i))
        return 0

    def mine(core):
        return pl.ds(pl.multiple_of(core * 512, 128), 640)

    lax.fori_loop(0, 2, y_first, 0)
    pair = exchange(yp.at[:, mine(1 - c)], sib_y, 1)
    pair.start()
    y_tile(2 * c)
    pair.wait()
    ys[...] = yp[:, mine(c)] + sib_y[...]
    copies += scatter(ys, rsy, yrs_s, yrs_r)
    merges(3)
    completes(1)
    second_merges(0)
    merges(4)
    completes(2)

    products = mm(left3[...], left3[...], NT)
    gram = jnp.zeros((RANK, RANK), jnp.float32)
    for i in (2, 1, 0):
        for j in (2, 1, 0):
            gram = gram + products[i * RANK : (i + 1) * RANK, j * RANK : (j + 1) * RANK]
    row_id = lax.broadcasted_iota(jnp.int32, (RANK, 2 * RANK), 0)
    lane_id = lax.broadcasted_iota(jnp.int32, (RANK, 2 * RANK), 1)
    elim[:, 0:RANK] = gram
    elim[:, RANK:] = jnp.where(row_id[:, 0:RANK] == lane_id[:, 0:RANK], 1.0, 0.0)

    def eliminate(j, _):
        row = elim[pl.ds(j, 1), :]
        full = elim[...]
        pivot = jnp.sum(jnp.where(lane_id[0:1] == j, row, 0.0), axis=1, keepdims=True)
        column = jnp.sum(jnp.where(lane_id == j, full, 0.0), axis=1, keepdims=True)
        factor = jnp.where(row_id[:, 0:1] > j, column / pivot, 0.0)
        elim[...] = full - factor * row
        return 0

    lax.fori_loop(0, RANK - 1, eliminate, 0)

    total = ys[own_rows, :]
    for copy in copies[7:]:
        copy.wait_recv()
    for d in range(1, NZ):
        total = total + rsy[d]
    yf[own_rows, mine(c)] = total

    def y_given(j, core):
        return yf.at[pl.ds(aligned(j, 8), 8), pl.ds(pl.multiple_of(core * 640, 128), 512)]

    y_finish, y_taken, y_sent = gather(
        lambda j: yf.at[pl.ds(aligned(j, 8), 8), mine(c)], yag_s, yag_r, y_given, yfw_s, yfw_r
    )
    done = elim[...]
    diagonal = jnp.sum(jnp.where(lane_id == row_id, done, 0.0), axis=1, keepdims=True)
    inverse = done[:, RANK:] / jnp.sqrt(diagonal)
    k = dp % 8
    window = left[dp // 8, :, pl.ds(aligned(k, 128), 256)]
    own_left = pltpu.roll(window, (256 - 16 * k) % 256, 1)[:, 0:CHUNK]
    own_basis = mm32(inverse, own_left, NN)
    second_merges(1)
    completes(3)
    second_merges(2)
    y_finish()
    completes(4)
    second_merges(3)
    y_taken()
    loads[4].wait()
    for t in range(3):
        columns = pl.ds(t * TILE, TILE)
        right = mm32(inverse, yf[:, columns], NN) * (1.0 / NDP)
        right_ref[:, columns] = right
        mom_ref[:, columns] = DECAY * momentum[:, columns] + mm32(own_basis, right, TN)
    second_merges(4)
    feature_finish()

    for copy in copies:
        copy.wait_send()
    sent()
    y_sent()
    for s in range(5):
        for way in (0, 1):
            if s < 4:
                ring_copy(way, s + 1).wait_send()
            if way in ways_of(s):
                pair_copy(way, s, c).wait_send()

    def drain(j, _):
        for h in range(2):
            first.drain(h, j)
        return 0

    lax.fori_loop(0, NDP, drain, 0)

    def drain_second(k, _):
        for h in range(2):
            second.drain(h, own_block(h, k))
        return 0

    lax.fori_loop(0, 4, drain_second, 0)


def fused(tokens, cot, weight, carried, momentum, q_t):
    f32, bf16 = jnp.float32, jnp.bfloat16
    dma = pltpu.SemaphoreType.DMA
    hbm = pl.BlockSpec(memory_space=pl.ANY)
    vmem = pl.BlockSpec(memory_space=pltpu.VMEM)
    return pl.pallas_call(
        fused_kernel,
        out_shape=(
            jax.ShapeDtypeStruct((CHUNK, 768), f32),
            jax.ShapeDtypeStruct((RANK, 1152), f32),
            jax.ShapeDtypeStruct((CHUNK, 1152), f32),
        ),
        in_specs=[hbm] * 5 + [vmem],
        out_specs=(vmem, vmem, vmem),
        scratch_shapes=[
            pltpu.VMEM((768, 2304), bf16),
            pltpu.VMEM((768, 1152), bf16),
            pltpu.VMEM((2304, 1152), bf16),
            pltpu.VMEM((CHUNK, 1152), f32),
            pltpu.VMEM((192, 1152), bf16),
            pltpu.VMEM((192, 768), bf16),
            pltpu.VMEM((2, RANK, 1152), f32),
            pltpu.VMEM((RANK, 1152), f32),
            pltpu.VMEM((RANK, 1152), f32),
            pltpu.VMEM((NZ, 8, 1152), f32),
            pltpu.VMEM((2, RANK, 1152), f32),
            pltpu.VMEM((192, 2304), bf16),
            pltpu.VMEM((RANK, 1152), f32),
            pltpu.VMEM((RANK, 640), f32),
            pltpu.VMEM((RANK, 640), f32),
            pltpu.VMEM((NZ, 8, 640), f32),
            pltpu.VMEM((RANK, 1152), f32),
            pltpu.VMEM((RANK, 128), f32),
            pltpu.VMEM((2304, 1152), bf16),
            pltpu.VMEM((2, 2304, TILE), f32),
            pltpu.VMEM((2, 2, 4, CHUNK, TILE), f32),
            pltpu.VMEM((2, 2, 4, HALF, TILE), f32),
            pltpu.VMEM((2, 2, 1, CHUNK, TILE), f32),
            pltpu.VMEM((2, 2, 1, HALF, TILE), f32),
            dma((5,)),
            dma((4,)),
        ]
        + [dma((NZ,))] * 12
        + [
            dma((2, 5)),
            dma((2, 5)),
            dma((2, 5)),
            dma((2, 5)),
            dma((2, NDP, 2)),
            dma((2, 2, 4, 2)),
            dma((2, 2, 4)),
            dma((2, NDP, 2)),
            dma((2, 2, 1, 2)),
            dma((2, 2, 1)),
        ],
        compiler_params=pltpu.CompilerParams(
            collective_id=0, has_side_effects=True, vmem_limit_bytes=56 * 2**20
        ),
        cost_estimate=pl.CostEstimate(
            flops=8 * 10**9, bytes_accessed=14 * 10**6, transcendentals=0
        ),
        name="fused",
    )(tokens, cot, weight, carried, momentum, q_t)


def hand_on_kernel(*refs):
    sources, results, held, sems = refs[0:3], refs[3:6], refs[6:9], refs[9]
    loads = [pltpu.make_async_copy(sources[i], held[i], sems.at[i]) for i in range(3)]
    stores = [pltpu.make_async_copy(held[i], results[i], sems.at[3 + i]) for i in range(3)]
    for copy in loads:
        copy.start()
    for load, store in zip(loads, stores):
        load.wait()
        store.start()
    for copy in stores:
        copy.wait()


def hand_on(*arrays):
    hbm = pl.BlockSpec(memory_space=pl.ANY)
    return pl.pallas_call(
        hand_on_kernel,
        out_shape=tuple(jax.ShapeDtypeStruct(a.shape, a.dtype) for a in arrays),
        in_specs=[hbm] * 3,
        out_specs=(hbm,) * 3,
        scratch_shapes=[pltpu.VMEM(a.shape, a.dtype) for a in arrays]
        + [pltpu.SemaphoreType.DMA((6,))],
        name="hand_on",
    )(*arrays)


def body(tokens, up_cotangent, up_weight, carried, momentum, q_start):
    feature_t, right_t, new_momentum = fused(
        tokens, up_cotangent, up_weight, carried[0], momentum, q_start.T
    )
    feature_t, right_t, new_momentum = hand_on(feature_t, right_t, new_momentum)
    return (feature_t.T, right_t.T, new_momentum)


def solution(mesh):
    placed = (
        P("dp", None),
        P("dp", "mp"),
        P("dp", "mp"),
        P("dp", None, "mp"),
        P("dp", "mp"),
        P("mp", None),
    )
    return jax.shard_map(
        body,
        mesh=mesh,
        in_specs=placed,
        out_specs=(P("dp", "mp"), P("mp", None), P("dp", "mp")),
        check_vma=False,
    )
```

```python
import jax
import jax.numpy as jnp
from jax import lax
from jax.experimental import pallas as pl
from jax.experimental.pallas import tpu as pltpu
from jax.sharding import PartitionSpec as P

DECAY = 0.9
MESH = pl.DeviceIdType.MESH
NT = (((1,), (1,)), ((), ()))
NN = (((1,), (0,)), ((), ()))
TN = (((0,), (0,)), ((), ()))
NZ = 8
NDP = 16
RANK = 64
TILE = 384
FAR_FIRST = (4, 3, 5, 2, 6, 1, 7)
NEAR_FIRST = (1, 7, 2, 6, 3, 5, 4)
CHUNK = 144
HALF = 72
SPLIT = 80


def mm(a, b, dims):
    return lax.dot_general(a, b, dims, preferred_element_type=jnp.float32)


def mm32(a, b, dims):
    return lax.dot_general(
        a, b, dims, precision=lax.Precision.HIGHEST, preferred_element_type=jnp.float32
    )


def split3(x):
    hi = x.astype(jnp.bfloat16)
    rest = x - hi.astype(jnp.float32)
    mid = rest.astype(jnp.bfloat16)
    low = (rest - mid.astype(jnp.float32)).astype(jnp.bfloat16)
    return jnp.concatenate([hi, mid, low], axis=0)


def fold3(x):
    return x[0:RANK] + x[RANK : 2 * RANK] + x[2 * RANK :]


def aligned(i, n):
    return pl.multiple_of(i * n, n)


def fused_kernel(
    tokens_hbm, cot_hbm, weight_hbm, carried_hbm, momentum_hbm, q_ref,
    feature_ref, right_ref, mom_ref,
    tokens, cot, carried, momentum, q3, t3, lp, sib_l, cs, rsl, left, left3,
    yp, sib_y, ys, rsy, yf, elim,
    weight, part, r1, rl1, r2, rl2,
    load_sem, sib_sem, rs_s, rs_r, ag_s, ag_r, yrs_s, yrs_r, yag_s, yag_r,
    fw_s, fw_r, yfw_s, yfw_r,
    w_s, w_r, ws_s, ws_r, f1_s, r1_r, rl1_r, f2_s, r2_r, rl2_r,
):
    dp = lax.axis_index("dp")
    mp = lax.axis_index("mp")
    z, c = dp // 2, dp % 2
    x, y = mp // 4, mp % 4
    sib = (z * 2 + 1 - c, mp)

    def zdev(d):
        return ((z + d) % NZ * 2 + c, mp)

    def xydev(axis, d):
        if axis == 0:
            return (dp, (x + d) % 4 * 4 + y)
        return (dp, x * 4 + (y + d) % 4)

    def remote(src, dst, send, recv, device):
        return pltpu.make_async_remote_copy(
            src_ref=src, dst_ref=dst, send_sem=send, recv_sem=recv,
            device_id=device, device_id_type=MESH,
        )

    own_chunk = pl.ds(pl.multiple_of(dp * CHUNK, 16), CHUNK)
    loads = [
        pltpu.make_async_copy(src, dst, load_sem.at[i])
        for i, (src, dst) in enumerate(
            (
                (weight_hbm, weight.at[own_chunk, :]), (cot_hbm, cot), (tokens_hbm, tokens),
                (carried_hbm, carried), (momentum_hbm, momentum),
            )
        )
    ]
    for copy in loads:
        copy.start()
    barrier = pltpu.get_barrier_semaphore()
    pl.semaphore_signal(barrier, inc=1, device_id=sib, device_id_type=MESH)
    for d in FAR_FIRST:
        pl.semaphore_signal(barrier, inc=1, device_id=zdev(d), device_id_type=MESH)
    for axis in range(2):
        for d in (1, 3):
            pl.semaphore_signal(barrier, inc=1, device_id=xydev(axis, d), device_id_type=MESH)

    def weight_rows(way, s, core, first=0, count=CHUNK):
        place = (z - s + NZ) % NZ if way == 0 else (z + s) % NZ
        return weight.at[pl.ds(pl.multiple_of((place * 2 + core) * CHUNK + first, 16), count), :]

    def ring_copy(way, s):
        first, count = 0, CHUNK
        if s == 4:
            first, count = (0, SPLIT) if way == 0 else (SPLIT, CHUNK - SPLIT)
        src = weight_rows(way, s - 1, c, first, count)
        return remote(src, src, w_s.at[way, s - 1], w_r.at[way, s], zdev(1 if way == 0 else NZ - 1))

    def ring_arrival(way, s):
        first, count = 0, CHUNK
        if s == 4:
            first, count = (0, SPLIT) if way == 0 else (SPLIT, CHUNK - SPLIT)
        dst = weight_rows(way, s, c, first, count)
        return remote(dst, dst, w_s.at[way, s - 1], w_r.at[way, s], zdev(1))

    def pair_copy(way, s, core):
        rows = weight_rows(way, s, core)
        return remote(rows, rows, ws_s.at[way, s], ws_r.at[way, s], sib)

    def ways_of(s):
        return (0,) if s in (0, 4) else (0, 1)

    def ring_step(s):
        for way in (0, 1):
            if s > 0:
                ring_arrival(way, s).wait_recv()
            if s < 4:
                ring_copy(way, s + 1).start()
            if s in (1, 2, 3):
                pair_copy(way, s, c).start()
        if s in (0, 4):
            pair_copy(0, s, c).start()

    def block(h, j, upper):
        return part.at[h, pl.ds(pl.multiple_of(j * CHUNK + (0 if upper else HALF), 8), HALF), :]

    def rows_of(upper):
        return pl.ds(0 if upper else HALF, HALF)

    class Stage:
        def __init__(self, number):
            self.number = number
            self.sends, self.arrive, self.passed = ((f1_s, r1_r, rl1_r), (f2_s, r2_r, rl2_r))[number]
            self.into, self.relay = ((r1, rl1), (r2, rl2))[number]

        def axis(self, h):
            return h if self.number == 0 else 1 - h

        def slot(self, h, j):
            if self.number == 1:
                return 0
            return j % 4 if h == 0 else j // 4

        def distance(self, h, j):
            if self.axis(h) == 0:
                return (j // 4 - x + 4) % 4
            return (j % 4 - y + 4) % 4

        def send(self, h, j, upper, direct, way):
            k = self.slot(h, j)
            source = block(h, j, upper)
            part_id = 0 if upper else 1
            if direct:
                dst = self.into.at[h, way, k, rows_of(upper), :]
                recv = self.arrive.at[h, way, k, part_id]
            else:
                dst = self.relay.at[h, way, k]
                recv = self.passed.at[h, way, k]
            return remote(
                source, dst, self.sends.at[h, j, part_id], recv,
                xydev(self.axis(h), 1 if way == 0 else 3),
            )

        def far(self, h, j):
            @pl.when(self.distance(h, j) == 2)
            def _():
                self.send(h, j, True, False, 0).start()
                self.send(h, j, False, False, 1).start()

        def near(self, h, j):
            far = self.distance(h, j)

            @pl.when(far == 1)
            def _():
                self.send(h, j, False, True, 0).start()

            @pl.when(far == 3)
            def _():
                self.send(h, j, True, True, 1).start()

        def merge(self, h, j):
            far = self.distance(h, j)
            k = self.slot(h, j)

            def one(way, upper):
                rows = block(h, j, upper)
                copy = remote(
                    self.relay.at[h, way, k], self.relay.at[h, way, k],
                    self.sends.at[h, j, 0], self.passed.at[h, way, k], xydev(self.axis(h), 1),
                )
                copy.wait_recv()
                rows[...] = rows[...] + self.relay[h, way, k]
                self.send(h, j, upper, True, way).start()

            @pl.when(far == 1)
            def _():
                one(0, True)

            @pl.when(far == 3)
            def _():
                one(1, False)

        def collect(self, h, j):
            k = self.slot(h, j)
            for way in range(2):
                for upper in (True, False):
                    dst = self.into.at[h, way, k, rows_of(upper), :]
                    remote(
                        dst, dst, self.sends.at[h, j, 0],
                        self.arrive.at[h, way, k, 0 if upper else 1], xydev(self.axis(h), 1),
                    ).wait_recv()
            own = pl.ds(pl.multiple_of(j * CHUNK, 8), CHUNK)
            return part[h, own, :] + self.into[h, 0, k] + self.into[h, 1, k]

        def drain(self, h, j):
            @pl.when(self.distance(h, j) != 0)
            def _():
                for upper in (True, False):
                    self.send(h, j, upper, True, 0).wait_send()

    first, second = Stage(0), Stage(1)

    def place_of(way, s):
        return (z - s + NZ) % NZ if way == 0 else (z + s) % NZ

    def units_of(s):
        for way in ways_of(s):
            for b in range(2):
                for h in range(2):
                    yield h, place_of(way, s) * 2 + b

    def partials(s):
        for way in ways_of(s):
            pair_copy(way, s, 1 - c).wait_recv()
            rows = pl.ds(pl.multiple_of(place_of(way, s) * (2 * CHUNK), 16), 2 * CHUNK)
            for h in range(2):
                part[h, rows, :] = mm(weight[rows, :], cot[pl.ds(h * TILE, TILE), :], NT)
        for h, j in units_of(s):
            first.far(h, j)
        for h, j in units_of(s):
            first.near(h, j)

    def merges(s):
        for h, j in units_of(s):
            first.merge(h, j)

    def completes(s):
        for h, j in units_of(s):

            @pl.when(first.distance(h, j) == 0)
            def _(h=h, j=j):
                part[h, pl.ds(pl.multiple_of(j * CHUNK, 8), CHUNK), :] = first.collect(h, j)
                second.far(h, j)
                second.near(h, j)

    def second_merges(s):
        for h, j in units_of(s):

            @pl.when(first.distance(h, j) == 0)
            def _(h=h, j=j):
                second.merge(h, j)

    def own_block(h, k):
        return x * 4 + k if h == 0 else k * 4 + y

    def feature_finish():
        for h in range(2):
            feature_ref[:, pl.ds(h * TILE, TILE)] = second.collect(h, mp)

    loads[0].wait()
    pl.semaphore_wait(barrier, NZ + 4)
    ring_step(0)
    loads[1].wait()
    partials(0)
    q3[...] = split3(q_ref[...])
    for t in range(2):
        rows = pl.ds(t * TILE, TILE)
        t3[:, rows] = split3(fold3(mm(q3[...], cot[rows, :], NT)))

    loads[2].wait()
    loads[3].wait()

    def left_half(h):
        def tile(t, _):
            columns = pl.ds(aligned(h * 3 + t, TILE), TILE)
            value = mm(q3[...], carried[columns, :], NT) + mm(t3[...], tokens[:, columns], NN)
            lp[h, :, pl.ds(aligned(t, TILE), TILE)] = fold3(value)
            return 0

        lax.fori_loop(0, 3, tile, 0)

    def exchange(src, dst, slot):
        return remote(src, dst, sib_sem.at[2 * slot], sib_sem.at[2 * slot + 1], sib)

    def scatter(src, dst, send, recv):
        copies = []
        for d in FAR_FIRST:
            copy = remote(
                src.at[pl.ds(aligned((z + d) % NZ, 8), 8), :], dst.at[d],
                send.at[d], recv.at[d], zdev(d),
            )
            copy.start()
            copies.append(copy)
        return copies

    def gather(block_of, send, recv, given_of, pass_send, pass_recv):
        copies = []
        for d in FAR_FIRST:
            copy = remote(block_of(z), block_of(z), send.at[d], recv.at[d], zdev(d))
            copy.start()
            copies.append(copy)

        def give(d):
            rows = given_of((z - d + NZ) % NZ, c)
            copy = remote(rows, rows, pass_send.at[d], pass_recv.at[d], sib)
            copy.start()
            copies.append(copy)

        give(0)

        def finish():
            for d in NEAR_FIRST:
                rows = block_of((z - d + NZ) % NZ)
                remote(rows, rows, send.at[d], recv.at[d], zdev(d)).wait_recv()
                give(d)

        def taken():
            for d in (0,) + NEAR_FIRST:
                rows = given_of((z - d + NZ) % NZ, 1 - c)
                remote(rows, rows, pass_send.at[d], pass_recv.at[d], sib).wait_recv()

        def sent():
            for copy in copies:
                copy.wait_send()

        return finish, taken, sent

    left_half(1 - c)
    pair = exchange(lp.at[1 - c], sib_l, 0)
    pair.start()
    ring_step(1)
    partials(1)
    left_half(c)
    pair.wait()
    cs[...] = lp[c] + sib_l[...]
    ring_step(2)
    partials(2)
    ring_step(3)
    copies = scatter(cs, rsl, rs_s, rs_r)
    merges(0)
    partials(3)
    merges(1)
    ring_step(4)
    partials(4)
    own_rows = pl.ds(aligned(z, 8), 8)
    total = cs[own_rows, :]
    for copy in copies:
        copy.wait_recv()
    for d in range(1, NZ):
        total = total + rsl[d]
    left[c, own_rows, :] = total * (1.0 / NDP)

    def left_block(j, core):
        return left.at[core, pl.ds(aligned(j, 8), 8), :]

    finish, taken, sent = gather(
        lambda j: left_block(j, c), ag_s, ag_r, left_block, fw_s, fw_r
    )
    merges(2)
    completes(0)
    finish()
    merges(3)
    merges(4)

    def half_columns(h):
        return pl.ds(aligned(h, 1152), 1152)

    left3[:, half_columns(c)] = split3(left[c])
    t2 = []
    for t in range(2):
        t2.append(
            mm(left3[:, half_columns(c)], tokens[pl.ds(t * TILE, TILE), half_columns(c)], NT)
        )
    taken()
    left3[:, half_columns(1 - c)] = split3(left[1 - c])
    for t in range(2):
        rows = pl.ds(t * TILE, TILE)
        rest = mm(left3[:, half_columns(1 - c)], tokens[rows, half_columns(1 - c)], NT)
        t3[:, rows] = split3(fold3(t2[t] + rest))

    def y_tile(t):
        columns = pl.ds(aligned(t, TILE), TILE)
        value = mm(left3[...], carried[:, columns], NN) + mm(t3[...], cot[:, columns], NN)
        yp[:, columns] = fold3(value)

    def y_first(i, _):
        y_tile(c * i + (1 - c) * (2 - i))
        return 0

    def mine(core):
        return pl.ds(pl.multiple_of(core * 512, 128), 640)

    lax.fori_loop(0, 2, y_first, 0)
    pair = exchange(yp.at[:, mine(1 - c)], sib_y, 1)
    pair.start()
    y_tile(2 * c)
    pair.wait()
    ys[...] = yp[:, mine(c)] + sib_y[...]
    copies += scatter(ys, rsy, yrs_s, yrs_r)
    completes(1)
    second_merges(0)
    completes(2)

    products = mm(left3[...], left3[...], NT)
    gram = jnp.zeros((RANK, RANK), jnp.float32)
    for i in (2, 1, 0):
        for j in (2, 1, 0):
            gram = gram + products[i * RANK : (i + 1) * RANK, j * RANK : (j + 1) * RANK]
    row_id = lax.broadcasted_iota(jnp.int32, (RANK, 2 * RANK), 0)
    lane_id = lax.broadcasted_iota(jnp.int32, (RANK, 2 * RANK), 1)
    elim[:, 0:RANK] = gram
    elim[:, RANK:] = jnp.where(row_id[:, 0:RANK] == lane_id[:, 0:RANK], 1.0, 0.0)

    def eliminate(j, _):
        row = elim[pl.ds(j, 1), :]
        full = elim[...]
        pivot = jnp.sum(jnp.where(lane_id[0:1] == j, row, 0.0), axis=1, keepdims=True)
        column = jnp.sum(jnp.where(lane_id == j, full, 0.0), axis=1, keepdims=True)
        factor = jnp.where(row_id[:, 0:1] > j, column / pivot, 0.0)
        elim[...] = full - factor * row
        return 0

    lax.fori_loop(0, RANK - 1, eliminate, 0)

    total = ys[own_rows, :]
    for copy in copies[7:]:
        copy.wait_recv()
    for d in range(1, NZ):
        total = total + rsy[d]
    yf[own_rows, mine(c)] = total

    def y_given(j, core):
        return yf.at[pl.ds(aligned(j, 8), 8), pl.ds(pl.multiple_of(core * 640, 128), 512)]

    y_finish, y_taken, y_sent = gather(
        lambda j: yf.at[pl.ds(aligned(j, 8), 8), mine(c)], yag_s, yag_r, y_given, yfw_s, yfw_r
    )
    done = elim[...]
    diagonal = jnp.sum(jnp.where(lane_id == row_id, done, 0.0), axis=1, keepdims=True)
    inverse = done[:, RANK:] / jnp.sqrt(diagonal)
    k = dp % 8
    window = left[dp // 8, :, pl.ds(aligned(k, 128), 256)]
    own_left = pltpu.roll(window, (256 - 16 * k) % 256, 1)[:, 0:CHUNK]
    own_basis = mm32(inverse, own_left, NN)
    second_merges(1)
    completes(3)
    second_merges(2)
    y_finish()
    completes(4)
    second_merges(3)
    y_taken()
    loads[4].wait()
    for t in range(3):
        columns = pl.ds(t * TILE, TILE)
        right = mm32(inverse, yf[:, columns], NN) * (1.0 / NDP)
        right_ref[:, columns] = right
        mom_ref[:, columns] = DECAY * momentum[:, columns] + mm32(own_basis, right, TN)
    second_merges(4)
    feature_finish()

    for copy in copies:
        copy.wait_send()
    sent()
    y_sent()
    for s in range(5):
        for way in (0, 1):
            if s < 4:
                ring_copy(way, s + 1).wait_send()
            if way in ways_of(s):
                pair_copy(way, s, c).wait_send()

    def drain(j, _):
        for h in range(2):
            first.drain(h, j)
        return 0

    lax.fori_loop(0, NDP, drain, 0)

    def drain_second(k, _):
        for h in range(2):
            second.drain(h, own_block(h, k))
        return 0

    lax.fori_loop(0, 4, drain_second, 0)


def fused(tokens, cot, weight, carried, momentum, q_t):
    f32, bf16 = jnp.float32, jnp.bfloat16
    dma = pltpu.SemaphoreType.DMA
    hbm = pl.BlockSpec(memory_space=pl.ANY)
    vmem = pl.BlockSpec(memory_space=pltpu.VMEM)
    return pl.pallas_call(
        fused_kernel,
        out_shape=(
            jax.ShapeDtypeStruct((CHUNK, 768), f32),
            jax.ShapeDtypeStruct((RANK, 1152), f32),
            jax.ShapeDtypeStruct((CHUNK, 1152), f32),
        ),
        in_specs=[hbm] * 5 + [vmem],
        out_specs=(vmem, vmem, vmem),
        scratch_shapes=[
            pltpu.VMEM((768, 2304), bf16),
            pltpu.VMEM((768, 1152), bf16),
            pltpu.VMEM((2304, 1152), bf16),
            pltpu.VMEM((CHUNK, 1152), f32),
            pltpu.VMEM((192, 1152), bf16),
            pltpu.VMEM((192, 768), bf16),
            pltpu.VMEM((2, RANK, 1152), f32),
            pltpu.VMEM((RANK, 1152), f32),
            pltpu.VMEM((RANK, 1152), f32),
            pltpu.VMEM((NZ, 8, 1152), f32),
            pltpu.VMEM((2, RANK, 1152), f32),
            pltpu.VMEM((192, 2304), bf16),
            pltpu.VMEM((RANK, 1152), f32),
            pltpu.VMEM((RANK, 640), f32),
            pltpu.VMEM((RANK, 640), f32),
            pltpu.VMEM((NZ, 8, 640), f32),
            pltpu.VMEM((RANK, 1152), f32),
            pltpu.VMEM((RANK, 128), f32),
            pltpu.VMEM((2304, 1152), bf16),
            pltpu.VMEM((2, 2304, TILE), f32),
            pltpu.VMEM((2, 2, 4, CHUNK, TILE), f32),
            pltpu.VMEM((2, 2, 4, HALF, TILE), f32),
            pltpu.VMEM((2, 2, 1, CHUNK, TILE), f32),
            pltpu.VMEM((2, 2, 1, HALF, TILE), f32),
            dma((5,)),
            dma((4,)),
        ]
        + [dma((NZ,))] * 12
        + [
            dma((2, 5)),
            dma((2, 5)),
            dma((2, 5)),
            dma((2, 5)),
            dma((2, NDP, 2)),
            dma((2, 2, 4, 2)),
            dma((2, 2, 4)),
            dma((2, NDP, 2)),
            dma((2, 2, 1, 2)),
            dma((2, 2, 1)),
        ],
        compiler_params=pltpu.CompilerParams(
            collective_id=0, has_side_effects=True, vmem_limit_bytes=56 * 2**20
        ),
        cost_estimate=pl.CostEstimate(
            flops=8 * 10**9, bytes_accessed=14 * 10**6, transcendentals=0
        ),
        name="fused",
    )(tokens, cot, weight, carried, momentum, q_t)


def hand_on_kernel(*refs):
    sources, results, held, sems = refs[0:3], refs[3:6], refs[6:9], refs[9]
    loads = [pltpu.make_async_copy(sources[i], held[i], sems.at[i]) for i in range(3)]
    stores = [pltpu.make_async_copy(held[i], results[i], sems.at[3 + i]) for i in range(3)]
    for copy in loads:
        copy.start()
    for load, store in zip(loads, stores):
        load.wait()
        store.start()
    for copy in stores:
        copy.wait()


def hand_on(*arrays):
    hbm = pl.BlockSpec(memory_space=pl.ANY)
    return pl.pallas_call(
        hand_on_kernel,
        out_shape=tuple(jax.ShapeDtypeStruct(a.shape, a.dtype) for a in arrays),
        in_specs=[hbm] * 3,
        out_specs=(hbm,) * 3,
        scratch_shapes=[pltpu.VMEM(a.shape, a.dtype) for a in arrays]
        + [pltpu.SemaphoreType.DMA((6,))],
        name="hand_on",
    )(*arrays)


def body(tokens, up_cotangent, up_weight, carried, momentum, q_start):
    feature_t, right_t, new_momentum = fused(
        tokens, up_cotangent, up_weight, carried[0], momentum, q_start.T
    )
    feature_t, right_t, new_momentum = hand_on(feature_t, right_t, new_momentum)
    return (feature_t.T, right_t.T, new_momentum)


def solution(mesh):
    placed = (
        P("dp", None),
        P("dp", "mp"),
        P("dp", "mp"),
        P("dp", None, "mp"),
        P("dp", "mp"),
        P("mp", None),
    )
    return jax.shard_map(
        body,
        mesh=mesh,
        in_specs=placed,
        out_specs=(P("dp", "mp"), P("mp", None), P("dp", "mp")),
        check_vma=False,
    )
```
